512 devices in a mesh: resp: 8 (over y), fsdp: 64 (over x, z, core).
Axes of the slice: x: 4, y: 8, z: 8, core: 2. Of those that a mesh axis runs over, the one named last changes fastest.
Arguments:
- queries: bfloat16 [64, 1024, 2560], P('fsdp', 'resp'), may hold values from -130 to 130
- resp_keys: bfloat16 [64, 1024, 512], P('fsdp', 'resp'), may hold values from -6 to 6
- response_values: bfloat16 [64, 1024, 512], P('fsdp', 'resp'), may hold values from -6 to 6
- rotated_prompt_keys: bfloat16 [64, 128, 512], P('fsdp', 'resp'), may hold values from -6 to 6
- prompt_value_rows: bfloat16 [64, 128, 512], P('fsdp', 'resp'), may hold values from -6 to 6
- attention_output_gradient: bfloat16 [64, 1024, 2560], P('fsdp', 'resp'), may hold values from -6 to 6
- output_grad: bfloat16 [64, 1024, 5120], P('fsdp', 'resp'), may hold values from -6 to 6
- advantages: float32 [64, 8], P('fsdp', 'resp'), may hold values from -4 to 4
- lengths: int32 [64, 8], P('fsdp'), may hold values from 1 to 128, as said below
- tree_mask: int32 [64, 16, 16], P('fsdp'), may hold values from 0 to 1, as said below
- adapter: float32 [16, 7680], P(None, 'fsdp'), may hold values from -0.3 to 0.3
- first_moment: float32 [16, 7680], P(None, 'fsdp'), may hold values from -0.013671875 to 0.013671875
- second_moment: float32 [16, 7680], P(None, 'fsdp'), may hold values from 1.6276042e-09 to 1.6276041e-07
Outputs:
- query_grad: bfloat16 [64, 1024, 2560], P('fsdp', 'resp')
- key_grad: bfloat16 [64, 1024, 512], P('fsdp', 'resp')
- value_grad: bfloat16 [64, 1024, 512], P('fsdp', 'resp')
- prompt_key_grad: bfloat16 [64, 128, 512], P('fsdp', 'resp')
- prompt_value_grad: bfloat16 [64, 128, 512], P('fsdp', 'resp')
- adam_update: float32 [16, 7680], P(None, 'fsdp')
The draws below stay inside these ranges and needn't reach their ends.
Inputs may be any that keep to these rules, and one draw needn't show every extreme that they name: `lengths`: in every group some response has exactly 128 tokens. Each group's blocks form a forest: every block but a response's first hangs on the block before it, a response's first block hangs on no block or on a block of a lower-numbered response of its group; tree_mask[g, b, c] is 1 where c is b or one of its ancestors, else 0.
All inputs are finite; a program needn't handle non-finite values.
Results may differ from the reference program's by a relative error of at most 0.018.
Values may be sent and summed in bfloat16 or wider, within the bound.
No kernel may reach another device: no remote copies, remote signals or barrier semaphores. Data moves between devices by JAX's collectives and lax.ppermute only.
A program may use at most 128 MiB of HBM per device.

```python
import math
import jax
import jax.numpy as jnp
from jax import lax

D = 5120
HEAD_SIZE = 128
QUERY_HEADS = 20
KEY_VALUE_HEADS = 4
RANK = 16
BLK = 64
RESPONSE_TOKENS = 128
PRE_DEV = 16
GROUP_TOKENS = 1024
PROMPT_TOKENS = 128
NBLK = 16
WIDE = 7680
N_RESP = 8
N_FSDP = 64


def key_rows(key):
    return jnp.clip(jax.random.normal(key, (N_FSDP, N_RESP * RESPONSE_TOKENS, KEY_VALUE_HEADS * HEAD_SIZE), jnp.float32), -6.0, 6.0)


def draw_resp_keys(key, part):
    shared_rows = key_rows(key)
    return shared_rows.astype(jnp.bfloat16)


def draw_queries(key, part):
    key = jax.random.fold_in(key, 12)
    complete_shape = (N_FSDP, N_RESP * RESPONSE_TOKENS, QUERY_HEADS * HEAD_SIZE)
    entries = jnp.clip(jax.random.normal(key, complete_shape, jnp.float32), -6.0, 6.0)
    return entries.astype(jnp.bfloat16)


def draw_lengths(key, part):
    key = jax.random.fold_in(key, 21)
    drawn = jax.random.randint(key, (N_FSDP, N_RESP), 1, RESPONSE_TOKENS + 1)
    longest = jax.random.randint(jax.random.fold_in(key, 1), (N_FSDP, 1), 0, N_RESP)
    column = jnp.arange(N_RESP, dtype=jnp.int32)[None, :]
    return jnp.where(column == longest, RESPONSE_TOKENS, drawn).astype(jnp.int32)


def draw_tree_mask(key, part):
    key = jax.random.fold_in(key, 31)
    per_resp = RESPONSE_TOKENS // BLK
    blocks = jnp.arange(NBLK, dtype=jnp.int32)
    owner = blocks // per_resp
    leading = blocks % per_resp == 0
    drawn = jax.random.randint(key, (N_FSDP, NBLK), 0, 1 << 20)
    parent = jnp.where(leading[None, :], drawn % (owner[None, :] * per_resp + 1) - 1, blocks[None, :] - 1)
    reach = (parent[:, :, None] == blocks[None, None, :]).astype(jnp.int32)
    for sweep in range(NBLK.bit_length()):
        reach = jnp.minimum(reach + jnp.matmul(reach, reach), 1)
    return jnp.minimum(reach + jnp.eye(NBLK, dtype=jnp.int32)[None], 1).astype(jnp.int32)


def block_levels(key, extent, shards, least, top_value):
    def one(dim, blocks):
        heights = jax.random.uniform(jax.random.fold_in(jax.random.fold_in(key, 6), dim), (blocks,), jnp.float32, least / len(shards), top_value / len(shards))
        return jnp.repeat(jnp.exp(heights), extent[dim] // blocks).reshape((-1,) + (1,) * (len(extent) - dim - 1))

    gain = one(*shards[0])
    for cut in shards[1:]:
        gain = gain * one(*cut)
    return gain


def bell_draw(rng, shape, spread, limit, cuts=(), kind=jnp.bfloat16):
    array = jax.random.normal(rng, shape, jnp.float32) * spread
    if len(cuts) > 0:
        array = block_levels(rng, shape, cuts, -0.22, 0.18) * array
    return jnp.clip(array, min=-limit, max=limit).astype(kind)


def setup_inputs(seed: int = 0) -> dict:
    key_of = jax.random.split(jax.random.key(seed), 14)
    return {
        "queries": draw_queries(jax.random.fold_in(key_of[13], 71), 0),
        "resp_keys": draw_resp_keys(jax.random.fold_in(key_of[13], 71), 0),
        "response_values": bell_draw(key_of[2], (N_FSDP, GROUP_TOKENS, KEY_VALUE_HEADS * HEAD_SIZE), 1.0, 6.0, ((0, 64), (1, 8))),
        "rotated_prompt_keys": bell_draw(key_of[3], (N_FSDP, PROMPT_TOKENS, KEY_VALUE_HEADS * HEAD_SIZE), 1.0, 6.0, ((0, 64), (1, 8))),
        "prompt_value_rows": bell_draw(key_of[4], (N_FSDP, PROMPT_TOKENS, KEY_VALUE_HEADS * HEAD_SIZE), 1.0, 6.0, ((0, 64), (1, 8))),
        "attention_output_gradient": bell_draw(key_of[5], (N_FSDP, GROUP_TOKENS, QUERY_HEADS * HEAD_SIZE), 1.0, 6.0, ((0, 64), (1, 8))),
        "output_grad": bell_draw(key_of[6], (N_FSDP, GROUP_TOKENS, D), 1.0, 6.0, ((0, 64), (1, 8))),
        "advantages": bell_draw(key_of[7], (N_FSDP, N_RESP), 1.0, 4.0, ((0, 64), (1, 8)), jnp.float32),
        "lengths": draw_lengths(jax.random.fold_in(key_of[13], 71), 0),
        "tree_mask": draw_tree_mask(jax.random.fold_in(key_of[13], 71), 0),
        "adapter": bell_draw(key_of[10], (RANK, WIDE), 0.05, 0.3, ((1, 64),), jnp.float32),
        "first_moment": bell_draw(key_of[11], (RANK, WIDE), (0.3 / (RANK * (QUERY_HEADS * HEAD_SIZE + D)) ** 0.5), 0.013671875, ((1, 64),), jnp.float32),
        "second_moment": jnp.clip(jnp.exp(math.log(1.627604149234685e-07) - 4.6051702 * jax.random.uniform(key_of[12], (RANK, WIDE), jnp.float32) ** block_levels(key_of[12], (RANK, WIDE), ((1, 64),), -0.2, 0.2)), 1.6276041625573612e-09, 1.627604149234685e-07),
    }


adapter_scale = 2.0
max_norm = 1.0
beta_first = 0.9
beta_second = 0.999
first_fix = 0.9999734386011124
second_fix = 0.0952078516
adam_eps = 1e-08

def visible(resp_index, lengths_row, tree_rows, n_resp, prefix_rows):
    per_resp = RESPONSE_TOKENS // BLK
    query_pos = jnp.arange(RESPONSE_TOKENS, dtype=jnp.int32)
    query_blk = resp_index * per_resp + query_pos // BLK
    key_col = jnp.arange(n_resp * RESPONSE_TOKENS, dtype=jnp.int32)
    key_pos = key_col % RESPONSE_TOKENS
    key_blk = key_col // BLK
    tree_bits = jnp.repeat(jnp.repeat(tree_rows, BLK, axis=1), BLK, axis=0)
    key_limit = jnp.repeat(lengths_row, RESPONSE_TOKENS)
    inside = (tree_bits == 1) & (key_pos[None, :] < key_limit[None, :])
    causal = (key_blk[None, :] != query_blk[:, None]) | (key_pos[None, :] <= query_pos[:, None])
    return jnp.concatenate([jnp.ones((RESPONSE_TOKENS, prefix_rows), jnp.bool_), inside & causal], axis=1)

def attend_heads(queries, all_keys, all_values, allowed, attention_cotangent):
    group_members = QUERY_HEADS // KEY_VALUE_HEADS
    score_scale = HEAD_SIZE ** (-0.5)
    outputs = []
    query_parts = []
    key_parts = []
    value_parts = []
    for current_head_index in range(KEY_VALUE_HEADS):
        columns = slice(current_head_index * group_members * HEAD_SIZE, (current_head_index + 1) * group_members * HEAD_SIZE)
        query_head = queries[:, columns].reshape(RESPONSE_TOKENS, group_members, HEAD_SIZE).astype(jnp.float32)
        grad_head = attention_cotangent[:, columns].reshape(RESPONSE_TOKENS, group_members, HEAD_SIZE).astype(jnp.float32)
        key_head = all_keys[:, current_head_index * HEAD_SIZE:(current_head_index + 1) * HEAD_SIZE].astype(jnp.float32)
        value_head = all_values[:, current_head_index * HEAD_SIZE:(current_head_index + 1) * HEAD_SIZE].astype(jnp.float32)
        scores = jnp.einsum('tgd,kd->gtk', query_head, key_head) * score_scale
        scores = jnp.where(allowed[None], scores, -jnp.inf)
        peak_value = lax.optimization_barrier(jnp.max(scores, axis=2, keepdims=True))
        row_total = lax.optimization_barrier(jnp.sum(jnp.exp(scores - peak_value), axis=2, keepdims=True))
        log_sum = peak_value + jnp.log(row_total)
        weights = jnp.exp(scores - log_sum)
        weight_half = weights.astype(jnp.bfloat16).astype(jnp.float32)
        head_out = jnp.einsum('gtk,kd->tgd', weight_half, value_head).astype(jnp.bfloat16)
        outputs.append(head_out.reshape(RESPONSE_TOKENS, group_members * HEAD_SIZE))
        out_head = head_out.astype(jnp.float32)
        value_parts.append(jnp.einsum('gtk,tgd->kd', weight_half, grad_head))
        weight_grad = jnp.einsum('tgd,kd->gtk', grad_head, value_head)
        inner = jnp.transpose(lax.optimization_barrier(jnp.sum(grad_head * out_head, axis=2)))[:, :, None]
        score_grad = (weights * (weight_grad - inner) * score_scale).astype(jnp.bfloat16).astype(jnp.float32)
        query_parts.append(jnp.einsum('gtk,kd->tgd', score_grad, key_head).reshape(RESPONSE_TOKENS, group_members * HEAD_SIZE))
        key_parts.append(jnp.einsum('gtk,tgd->kd', score_grad, query_head))
    return (jnp.concatenate(outputs, axis=1), jnp.concatenate(query_parts, axis=1), jnp.concatenate(key_parts, axis=1), jnp.concatenate(value_parts, axis=1))

def local_pass(queries, attention_output_gradient, output_grad, advantage, own_length, lengths_row, tree_rows, all_keys, all_values, adapter_down_input, low_out, resp_index, n_resp, prefix_rows):
    allowed = visible(resp_index, lengths_row, tree_rows, n_resp, prefix_rows)
    positions = jnp.arange(RESPONSE_TOKENS, dtype=jnp.int32)
    per_token_weight = jnp.where(positions < own_length, advantage / own_length.astype(jnp.float32), jnp.zeros((), jnp.float32))
    output_cotangent = (per_token_weight[:, None] * output_grad.astype(jnp.float32)).astype(jnp.bfloat16)
    down_projected = jnp.dot(output_cotangent, low_out.T, preferred_element_type=jnp.float32).astype(jnp.bfloat16)
    attention_cotangent = (per_token_weight[:, None] * attention_output_gradient.astype(jnp.float32) + adapter_scale * jnp.dot(down_projected, adapter_down_input, preferred_element_type=jnp.float32)).astype(jnp.bfloat16)
    attention_result_rows, query_grad, key_grad, value_grad = attend_heads(queries, all_keys, all_values, allowed, attention_cotangent)
    projected_rows = jnp.dot(attention_result_rows, adapter_down_input.T, preferred_element_type=jnp.float32).astype(jnp.bfloat16)
    input_gradient = adapter_scale * jnp.dot(down_projected.T, attention_result_rows, preferred_element_type=jnp.float32)
    output_gradient = adapter_scale * jnp.dot(projected_rows.T, output_cotangent, preferred_element_type=jnp.float32)
    adapter_grad = jnp.concatenate([input_gradient, output_gradient], axis=1)
    return (query_grad.astype(jnp.bfloat16), key_grad, value_grad, adapter_grad)

def adam_update_of(gradient, first_state, second_state, clip_factor):
    scaled = gradient * clip_factor
    moment = beta_first * first_state + (1.0 - beta_first) * scaled
    second_new = beta_second * second_state + (1.0 - beta_second) * scaled * scaled
    return moment / first_fix / (jnp.sqrt(second_new / second_fix) + adam_eps)

def reference(queries, resp_keys, response_values, rotated_prompt_keys, prompt_value_rows, attention_output_gradient, output_grad, advantages, lengths, tree_mask, adapter, first_moment, second_moment):
    split = QUERY_HEADS * HEAD_SIZE
    adapter_down_input = adapter[:, :split].astype(jnp.bfloat16)
    low_out = adapter[:, split:].astype(jnp.bfloat16)
    prefix_rows = N_RESP * PRE_DEV
    per_resp = RESPONSE_TOKENS // BLK

    def one_group(items):
        group_q, group_rk, group_rv, group_pk, group_pv, group_ag, group_og, group_adv, group_len, group_tree = items
        all_keys = jnp.concatenate([group_pk, group_rk], axis=0)
        all_values = jnp.concatenate([group_pv, group_rv], axis=0)

        def one_resp(resp_index):
            start = resp_index * RESPONSE_TOKENS
            tree_rows = lax.dynamic_slice_in_dim(group_tree, resp_index * per_resp, per_resp, 0)
            own_length = lax.dynamic_index_in_dim(group_len, resp_index, 0, keepdims=False)
            advantage = lax.dynamic_index_in_dim(group_adv, resp_index, 0, keepdims=False)
            query_grad, key_grad, value_grad, adapter_grad = local_pass(lax.dynamic_slice_in_dim(group_q, start, RESPONSE_TOKENS, 0), lax.dynamic_slice_in_dim(group_ag, start, RESPONSE_TOKENS, 0), lax.dynamic_slice_in_dim(group_og, start, RESPONSE_TOKENS, 0), advantage, own_length, group_len, tree_rows, all_keys, all_values, adapter_down_input, low_out, resp_index, N_RESP, prefix_rows)
            return (query_grad, key_grad.astype(jnp.bfloat16), value_grad.astype(jnp.bfloat16), adapter_grad)
        parts = lax.map(one_resp, jnp.arange(N_RESP, dtype=jnp.int32))
        key_total = lax.optimization_barrier(jnp.sum(parts[1].astype(jnp.float32), axis=0)).astype(jnp.bfloat16)
        value_total = lax.optimization_barrier(jnp.sum(parts[2].astype(jnp.float32), axis=0)).astype(jnp.bfloat16)
        return (parts[0].reshape(N_RESP * RESPONSE_TOKENS, split), key_total, value_total, lax.optimization_barrier(jnp.sum(parts[3], axis=0)))
    results = lax.map(one_group, (queries, resp_keys, response_values, rotated_prompt_keys, prompt_value_rows, attention_output_gradient, output_grad, advantages, lengths, tree_mask))
    adapter_grad = lax.optimization_barrier(jnp.sum(results[3], axis=0))
    squares = jnp.sum(adapter_grad * adapter_grad)
    clip_factor = max_norm / jnp.maximum(jnp.sqrt(squares), max_norm)
    update = adam_update_of(adapter_grad, first_moment, second_moment, clip_factor)
    return (results[0], results[1][:, prefix_rows:], results[2][:, prefix_rows:], results[1][:, :prefix_rows], results[2][:, :prefix_rows], update)
```

```python
import functools

import jax
import jax.numpy as jnp
from jax import lax
from jax.experimental import pallas as pl
from jax.experimental.pallas import tpu as pltpu
from jax.sharding import PartitionSpec as P

HEAD = 128
Q_HEADS = 20
KV_HEADS = 4
MEMBERS = Q_HEADS // KV_HEADS
BLK = 64
JOIN = 4
TOK = 128
PRE = 16
RANK = 16
LANES = 128

adapter_scale = 2.0
max_norm = 1.0
beta_first = 0.9
beta_second = 0.999
first_fix = 0.9999734386011124
second_fix = 0.0952078516
adam_eps = 1e-08

SCALE = HEAD ** (-0.5)
LOG2E = 1.4426950408889634
HIDDEN = -1e30

NT = (((1,), (1,)), ((), ()))
NN = (((1,), (0,)), ((), ()))
TN = (((0,), (0,)), ((), ()))


def dot(a, b, dims):
    return lax.dot_general(a, b, dims, preferred_element_type=jnp.float32)


def token_column(place_ref, lengths_ref, adv_ref):
    own = lengths_ref[0, place_ref[0]]
    weight = adv_ref[0, 0] / own.astype(jnp.float32)
    pos = lax.broadcasted_iota(jnp.int32, (TOK, LANES), 0)
    return jnp.where(pos < own, weight, 0.0)[:, :1]


def rows_of(i, size):
    return pl.ds(pl.multiple_of(i * size, size), size)


def block_rows(b2):
    per = TOK // BLK
    return pl.ds(pl.multiple_of((b2 // per) * (TOK + PRE) + PRE + (b2 % per) * BLK, PRE), BLK)


def block_bias(b2, r, lengths_ref, tree_ref):
    per = TOK // BLK
    r2 = b2 // per
    key_pos = (b2 % per) * BLK + lax.broadcasted_iota(jnp.int32, (BLK, TOK), 0)
    query_pos = lax.broadcasted_iota(jnp.int32, (BLK, TOK), 1)
    bit = jnp.where(query_pos < BLK, tree_ref[per * r, b2], tree_ref[per * r + 1, b2])
    reach = jnp.where(r2 == r, query_pos, TOK)
    seen = (bit == 1) & (key_pos < lengths_ref[0, r2]) & (key_pos <= reach)
    return jnp.where(seen, 0.0, HIDDEN)


def prepare_kernel(
    place_ref, lengths_ref, tree_ref, adv_ref, parts_ref, q_ref, og_ref, ag_ref,
    out_cot_ref, low_t_ref, low_in_ref, qs_ref, gs_ref, gt_ref, list_ref, bias_ref,
    whole_ref,
):
    n, _, _ = parts_ref.shape
    width = whole_ref.shape[1] // n
    for i in range(n):
        whole_ref[:, i * width : (i + 1) * width] = parts_ref[i, :, :width].astype(jnp.float32)
    split = ag_ref.shape[1]
    weight = token_column(place_ref, lengths_ref, adv_ref)
    out_cot_ref[...] = (weight * og_ref[...].astype(jnp.float32)).astype(jnp.bfloat16)
    low_in_ref[...] = whole_ref[:, :split].astype(jnp.bfloat16)
    low_out = whole_ref[:, split:].astype(jnp.bfloat16)
    low_t = dot(low_out, out_cot_ref[...], NT).astype(jnp.bfloat16)
    low_t_ref[...] = low_t
    for i in range(Q_HEADS):
        part = slice(i * HEAD, (i + 1) * HEAD)
        rows = slice(i * TOK, (i + 1) * TOK)
        added = adapter_scale * dot(low_t, low_in_ref[:, part], TN)
        grad = (weight * ag_ref[:, part].astype(jnp.float32) + added).astype(jnp.bfloat16)
        gs_ref[rows, :] = grad
        gt_ref[:, rows] = jnp.transpose(grad.astype(jnp.float32)).astype(jnp.bfloat16)
        qs_ref[rows, :] = q_ref[:, part]

    r = place_ref[0]
    per = TOK // BLK
    n_blocks = tree_ref.shape[1]
    first = n_blocks // per * PRE // BLK
    bias_ref[: first * BLK, :] = jnp.zeros((first * BLK, TOK), jnp.float32)

    def step(b2, count):
        bits = tree_ref[per * r, b2] + tree_ref[per * r + 1, b2]
        seen = (bits > 0) & ((b2 % per) * BLK < lengths_ref[0, b2 // per])

        @pl.when(seen)
        def _():
            list_ref[2 + count - first] = b2
            bias_ref[rows_of(count, BLK), :] = block_bias(b2, r, lengths_ref, tree_ref)

        return count + jnp.where(seen, 1, 0)

    count = lax.fori_loop(0, n_blocks, step, first)
    steps = (count + JOIN - 1) // JOIN
    list_ref[0] = count
    list_ref[1] = steps

    def hide(i, carry):
        bias_ref[rows_of(i, BLK), :] = jnp.full((BLK, TOK), HIDDEN, jnp.float32)
        return carry

    lax.fori_loop(count, steps * JOIN, hide, 0)


def places_of(n_blocks):
    places = n_blocks + n_blocks // (TOK // BLK) * PRE // BLK
    return -(-places // JOIN) * JOIN


def prepare(place, lengths, tree, advantages, parts, q, og, ag):
    smem = pl.BlockSpec(memory_space=pltpu.SMEM)
    vmem = pl.BlockSpec(memory_space=pltpu.VMEM)
    split = ag.shape[1]
    wide = split + og.shape[1]
    n_blocks = tree.shape[1]
    return pl.pallas_call(
        prepare_kernel,
        out_shape=(
            jax.ShapeDtypeStruct(og.shape, jnp.bfloat16),
            jax.ShapeDtypeStruct((RANK, TOK), jnp.bfloat16),
            jax.ShapeDtypeStruct((RANK, split), jnp.bfloat16),
            jax.ShapeDtypeStruct((split, HEAD), jnp.bfloat16),
            jax.ShapeDtypeStruct((split, HEAD), jnp.bfloat16),
            jax.ShapeDtypeStruct((HEAD, split), jnp.bfloat16),
            jax.ShapeDtypeStruct((n_blocks + 2,), jnp.int32),
            jax.ShapeDtypeStruct((places_of(n_blocks) * BLK, TOK), jnp.float32),
        ),
        in_specs=[smem] * 4 + [vmem] * 4,
        out_specs=[vmem] * 6 + [smem, vmem],
        scratch_shapes=[pltpu.VMEM((RANK, wide), jnp.float32)],
        compiler_params=pltpu.CompilerParams(vmem_limit_bytes=16 * 1024 * 1024),
        cost_estimate=pl.CostEstimate(flops=80_000_000, bytes_accessed=6_000_000, transcendentals=0),
        name="prepare",
    )(place, lengths, tree, advantages, parts, q, og, ag)


def spread(bias):
    return jnp.concatenate([bias] * MEMBERS, axis=1)


def fold(x, op):
    return op(x.reshape(x.shape[0] // 8, 8, x.shape[1]), axis=0)


def attend_kernel(
    list_ref, bias_hbm, qs_hbm, gs_hbm, gt_hbm, kv_ref,
    out_ref, turned_ref, kv_grad_ref,
    bias_ref, qs_ref, gs_ref, gt_ref, keys_ref, score_ref, acc_ref, peak_ref, total_ref, inner_ref,
    sums_ref, zero_ref,
    in_sem, place_sem, prompt_in_sem, prompt_sem, block_sem,
):
    c = SCALE * LOG2E
    n_blocks = block_sem.shape[0]
    n_resp = prompt_sem.shape[0]
    first = n_resp * PRE // BLK
    group = MEMBERS * TOK
    v0 = KV_HEADS * HEAD
    width = JOIN * BLK
    count = list_ref[0]
    steps = list_ref[1]

    def load(src, dst, i):
        return pltpu.make_async_copy(src, dst, in_sem.at[i])

    load_q, load_bias, load_g, load_gt = (
        load(qs_hbm, qs_ref, 0), load(bias_hbm, bias_ref, 1), load(gs_hbm, gs_ref, 2), load(gt_hbm, gt_ref, 3)
    )
    prompt_in = [
        pltpu.make_async_copy(
            kv_ref.at[pl.ds(i * (TOK + PRE), PRE)], keys_ref.at[pl.ds(i * PRE, PRE)], prompt_in_sem.at[i]
        )
        for i in range(n_resp)
    ]

    def bring(i):
        b2 = list_ref[2 + i - first]
        return pltpu.make_async_copy(kv_ref.at[block_rows(b2)], keys_ref.at[rows_of(i, BLK)], place_sem.at[i])

    def start(i, carry):
        bring(i).start()
        return carry

    for copy in prompt_in:
        copy.start()
    load_q.start()
    lax.fori_loop(first, count, start, 0)
    load_bias.start()
    load_g.start()
    load_gt.start()

    zero_ref[...] = jnp.zeros_like(zero_ref)
    peak_ref[...] = jnp.full_like(peak_ref, HIDDEN)
    total_ref[...] = jnp.zeros_like(total_ref)
    acc_ref[...] = jnp.zeros_like(acc_ref)

    def blank(i, carry):
        keys_ref[rows_of(i, BLK), :] = jnp.zeros((BLK, keys_ref.shape[1]), jnp.bfloat16)
        return carry

    lax.fori_loop(count, steps * JOIN, blank, 0)

    def block_out(src, b2):
        return pltpu.make_async_copy(src, kv_grad_ref.at[block_rows(b2)], block_sem.at[b2])

    def unseen(b2, at):
        hit = (at < count) & (list_ref[jnp.minimum(2 + at - first, n_blocks + 1)] == b2)

        @pl.when(jnp.logical_not(hit))
        def _():
            block_out(zero_ref, b2).start()

        return at + jnp.where(hit, 1, 0)

    lax.fori_loop(0, n_blocks, unseen, first)
    for copy in prompt_in:
        copy.wait()
    load_q.wait()
    load_bias.wait()

    def cols(h):
        return slice(h * group, (h + 1) * group)

    def score_step(i, carry):
        def arrive(at, carry):
            bring(at).wait()
            return carry

        lax.fori_loop(jnp.maximum(i * JOIN, first), jnp.minimum((i + 1) * JOIN, count), arrive, 0)
        rows = rows_of(i, width)
        bias = spread(bias_ref[rows, :])
        for h in range(KV_HEADS):
            s = dot(keys_ref[rows, h * HEAD : (h + 1) * HEAD], qs_ref[cols(h), :], NT) + bias
            score_ref[rows, cols(h)] = s
            peak_ref[:, cols(h)] = jnp.maximum(peak_ref[:, cols(h)], fold(s, jnp.max))
        return carry

    lax.fori_loop(0, steps, score_step, 0)
    peak = jnp.max(peak_ref[...], axis=0, keepdims=True) * c
    peak_ref[...] = jnp.broadcast_to(peak, peak_ref.shape)

    def value_step(i, carry):
        rows = rows_of(i, width)
        for h in range(KV_HEADS):
            e = jnp.exp2(score_ref[rows, cols(h)] * c - peak_ref[:1, cols(h)])
            score_ref[rows, cols(h)] = e
            total_ref[:, cols(h)] += fold(e, jnp.sum)
            v = keys_ref[rows, v0 + h * HEAD : v0 + (h + 1) * HEAD]
            acc_ref[:, cols(h)] += dot(v, e.astype(jnp.bfloat16), TN)
        return carry

    lax.fori_loop(0, steps, value_step, 0)
    inverse = 1.0 / jnp.sum(total_ref[...], axis=0, keepdims=True)
    total_ref[...] = jnp.broadcast_to(inverse, total_ref.shape)
    load_g.wait()
    load_gt.wait()
    for i in range(Q_HEADS):
        part = slice(i * TOK, (i + 1) * TOK)
        rounded = (acc_ref[:, part] * inverse[:, part]).astype(jnp.bfloat16)
        out_ref[:, part] = rounded
        across = gt_ref[:, part].astype(jnp.float32) * rounded.astype(jnp.float32)
        inner_ref[:, part] = jnp.broadcast_to(jnp.sum(across, axis=0, keepdims=True), (8, TOK))
    acc_ref[...] = jnp.zeros_like(acc_ref)

    def back_step(i, carry):
        rows = rows_of(i, width)
        for h in range(KV_HEADS):
            kc = slice(h * HEAD, (h + 1) * HEAD)
            vc = slice(v0 + h * HEAD, v0 + (h + 1) * HEAD)
            w = score_ref[rows, cols(h)] * total_ref[:1, cols(h)]
            across = dot(keys_ref[rows, vc], gs_ref[cols(h), :], NT)
            sums_ref[rows, vc] = dot(w.astype(jnp.bfloat16), gs_ref[cols(h), :], NN).astype(jnp.bfloat16)
            ds = (w * (across - inner_ref[:1, cols(h)])).astype(jnp.bfloat16)
            sums_ref[rows, kc] = (dot(ds, qs_ref[cols(h), :], NN) * SCALE).astype(jnp.bfloat16)
            acc_ref[:, cols(h)] += dot(keys_ref[rows, kc], ds, TN)

        def send(at, carry):
            block_out(sums_ref.at[rows_of(at, BLK)], list_ref[2 + at - first]).start()
            return carry

        lax.fori_loop(jnp.maximum(i * JOIN, first), jnp.minimum((i + 1) * JOIN, count), send, 0)
        return carry

    lax.fori_loop(0, steps, back_step, 0)
    prompts = [
        pltpu.make_async_copy(
            sums_ref.at[pl.ds(i * PRE, PRE)], kv_grad_ref.at[pl.ds(i * (TOK + PRE), PRE)], prompt_sem.at[i]
        )
        for i in range(n_resp)
    ]
    for copy in prompts:
        copy.start()
    turned_ref[...] = (acc_ref[...] * SCALE).astype(jnp.bfloat16)
    for copy in prompts:
        copy.wait()

    def finished(b2, carry):
        block_out(zero_ref, b2).wait()
        return carry

    lax.fori_loop(0, n_blocks, finished, 0)


def attend(blocks, bias, qs, gs, gt, kv, n_resp):
    smem = pl.BlockSpec(memory_space=pltpu.SMEM)
    vmem = pl.BlockSpec(memory_space=pltpu.VMEM)
    hbm = pl.BlockSpec(memory_space=pl.ANY)
    split = qs.shape[0]
    rows, columns = bias.shape[0], kv.shape[1]
    return pl.pallas_call(
        attend_kernel,
        out_shape=(
            jax.ShapeDtypeStruct((HEAD, split), jnp.bfloat16),
            jax.ShapeDtypeStruct((HEAD, split), jnp.bfloat16),
            jax.ShapeDtypeStruct(kv.shape, jnp.bfloat16),
        ),
        in_specs=[smem] + [hbm] * 5,
        out_specs=[vmem, vmem, hbm],
        scratch_shapes=[
            pltpu.VMEM(bias.shape, jnp.float32),
            pltpu.VMEM(qs.shape, jnp.bfloat16),
            pltpu.VMEM(gs.shape, jnp.bfloat16),
            pltpu.VMEM(gt.shape, jnp.bfloat16),
            pltpu.VMEM((rows, columns), jnp.bfloat16),
            pltpu.VMEM((rows, split), jnp.float32),
            pltpu.VMEM((HEAD, split), jnp.float32),
            pltpu.VMEM((8, split), jnp.float32),
            pltpu.VMEM((8, split), jnp.float32),
            pltpu.VMEM((8, split), jnp.float32),
            pltpu.VMEM((rows, columns), jnp.bfloat16),
            pltpu.VMEM((BLK, columns), jnp.bfloat16),
            pltpu.SemaphoreType.DMA((4,)),
            pltpu.SemaphoreType.DMA((rows // BLK,)),
            pltpu.SemaphoreType.DMA((n_resp,)),
            pltpu.SemaphoreType.DMA((n_resp,)),
            pltpu.SemaphoreType.DMA((n_resp * (TOK // BLK),)),
        ],
        compiler_params=pltpu.CompilerParams(vmem_limit_bytes=56 * 1024 * 1024),
        cost_estimate=pl.CostEstimate(
            flops=3_800_000_000, bytes_accessed=8_000_000, transcendentals=3_000_000
        ),
        name="attend",
    )(blocks, bias, qs, gs, gt, kv)


def pieces_kernel(out_t_ref, low_t_ref, low_in_ref, out_cot_ref, parts_ref, wide_ref):
    projected_t = jnp.zeros((RANK, TOK), jnp.float32)
    for i in range(Q_HEADS):
        part = slice(i * TOK, (i + 1) * TOK)
        projected_t += dot(low_in_ref[:, part], out_t_ref[:, part], NN)
        wide_ref[:, part] = adapter_scale * dot(low_t_ref[...], out_t_ref[:, part], NT)
    split = out_t_ref.shape[1]
    wide_ref[:, split:] = adapter_scale * dot(projected_t.astype(jnp.bfloat16), out_cot_ref[...], NN)
    parts_ref[...] = jnp.zeros_like(parts_ref)
    n_parts = parts_ref.shape[0]
    piece = wide_ref.shape[1] // n_parts
    for i in range(n_parts):
        parts_ref[i, :, :piece] = wide_ref[:, i * piece : (i + 1) * piece].astype(jnp.bfloat16)


PIECES_FLOPS = 200_000_000_000


def pieces(out_t, low_t, low_in, out_cot, n_fsdp):
    vmem = pl.BlockSpec(memory_space=pltpu.VMEM)
    wide = out_t.shape[1] + out_cot.shape[1]
    return pl.pallas_call(
        pieces_kernel,
        out_shape=jax.ShapeDtypeStruct((n_fsdp, RANK, LANES), jnp.bfloat16),
        in_specs=[vmem] * 4,
        out_specs=vmem,
        scratch_shapes=[pltpu.VMEM((RANK, wide), jnp.float32)],
        cost_estimate=pl.CostEstimate(flops=PIECES_FLOPS, bytes_accessed=2_500_000, transcendentals=0),
        name="pieces",
    )(out_t, low_t, low_in, out_cot)


def turn_kernel(turned_ref, out_ref):
    for i in range(Q_HEADS):
        part = slice(i * TOK, (i + 1) * TOK)
        out_ref[:, part] = jnp.transpose(turned_ref[:, part].astype(jnp.float32)).astype(jnp.bfloat16)


def turn(turned):
    vmem = pl.BlockSpec(memory_space=pltpu.VMEM)
    return pl.pallas_call(
        turn_kernel,
        out_shape=jax.ShapeDtypeStruct((TOK, turned.shape[1]), jnp.bfloat16),
        in_specs=[vmem],
        out_specs=vmem,
        cost_estimate=pl.CostEstimate(flops=1_000_000, bytes_accessed=1_300_000, transcendentals=0),
        name="turn",
    )(turned)


def pack_kernel(rk_ref, rv_ref, pk_ref, pv_ref, own_ref):
    half = rk_ref.shape[2]
    own_ref[:PRE, :half] = pk_ref[0]
    own_ref[:PRE, half:] = pv_ref[0]
    own_ref[PRE:, :half] = rk_ref[0]
    own_ref[PRE:, half:] = rv_ref[0]


def pack(rk, rv, pk, pv):
    vmem = pl.BlockSpec(memory_space=pltpu.VMEM)
    return pl.pallas_call(
        pack_kernel,
        out_shape=jax.ShapeDtypeStruct((PRE + rk.shape[1], 2 * rk.shape[2]), jnp.bfloat16),
        in_specs=[vmem] * 4,
        out_specs=vmem,
        cost_estimate=pl.CostEstimate(flops=1_000, bytes_accessed=600_000, transcendentals=0),
        name="pack",
    )(rk, rv, pk, pv)


def shards_kernel(adapter_ref, parts_ref):
    width = adapter_ref.shape[1]
    parts_ref[0] = jnp.zeros(parts_ref.shape[1:], jnp.bfloat16)
    parts_ref[0, :, :width] = adapter_ref[...].astype(jnp.bfloat16)
    shard = parts_ref[0]
    for i in range(1, parts_ref.shape[0]):
        parts_ref[i] = shard


def shards(adapter, n_fsdp):
    vmem = pl.BlockSpec(memory_space=pltpu.VMEM)
    return pl.pallas_call(
        shards_kernel,
        out_shape=jax.ShapeDtypeStruct((n_fsdp, RANK, LANES), jnp.bfloat16),
        in_specs=[vmem],
        out_specs=vmem,
        cost_estimate=pl.CostEstimate(flops=1_000, bytes_accessed=300_000, transcendentals=0),
        name="shards",
    )(adapter)


def group_sum_kernel(parts_ref, copies_ref):
    total = jnp.sum(parts_ref[...].astype(jnp.float32), axis=0)
    for i in range(copies_ref.shape[0]):
        copies_ref[i] = total


def group_sum(parts, copies):
    vmem = pl.BlockSpec(memory_space=pltpu.VMEM)
    return pl.pallas_call(
        group_sum_kernel,
        out_shape=jax.ShapeDtypeStruct((copies,) + parts.shape[1:], jnp.float32),
        in_specs=[vmem],
        out_specs=vmem,
        cost_estimate=pl.CostEstimate(flops=200_000, bytes_accessed=400_000, transcendentals=0),
        name="group_sum",
    )(parts)


def norm_kernel(parts_ref, owned_ref, squares_ref):
    owned = jnp.sum(parts_ref[...], axis=0)
    owned_ref[...] = owned
    squares = jnp.sum(jnp.sum(owned * owned, axis=0, keepdims=True), axis=1, keepdims=True)
    squares_ref[...] = jnp.broadcast_to(squares[None], squares_ref.shape)


def norm(parts, copies):
    vmem = pl.BlockSpec(memory_space=pltpu.VMEM)
    return pl.pallas_call(
        norm_kernel,
        out_shape=(
            jax.ShapeDtypeStruct(parts.shape[1:], jnp.float32),
            jax.ShapeDtypeStruct((copies, 1, LANES), jnp.float32),
        ),
        in_specs=[vmem],
        out_specs=[vmem] * 2,
        cost_estimate=pl.CostEstimate(flops=100_000, bytes_accessed=100_000, transcendentals=0),
        name="norm",
    )(parts)


def finish_kernel(
    kv_ref, owned_ref, squares_ref, first_ref, second_ref,
    rk_ref, rv_ref, pk_ref, pv_ref, update_ref,
):
    half = rk_ref.shape[2]
    rk_ref[0] = kv_ref[PRE:, :half]
    rv_ref[0] = kv_ref[PRE:, half:]
    pk_ref[0] = kv_ref[:PRE, :half]
    pv_ref[0] = kv_ref[:PRE, half:]
    width = first_ref.shape[1]
    squares = jnp.sum(squares_ref[...], axis=0)[:, :width]
    clip_factor = max_norm / jnp.maximum(jnp.sqrt(squares), max_norm)
    scaled = owned_ref[:, :width] * clip_factor
    moment = beta_first * first_ref[...] + (1.0 - beta_first) * scaled
    second_new = beta_second * second_ref[...] + (1.0 - beta_second) * scaled * scaled
    update_ref[...] = moment / first_fix / (jnp.sqrt(second_new / second_fix) + adam_eps)


def finish(kv_sum, owned, squares, first, second):
    vmem = pl.BlockSpec(memory_space=pltpu.VMEM)
    half = kv_sum.shape[1] // 2
    return pl.pallas_call(
        finish_kernel,
        out_shape=(
            jax.ShapeDtypeStruct((1, TOK, half), jnp.bfloat16),
            jax.ShapeDtypeStruct((1, TOK, half), jnp.bfloat16),
            jax.ShapeDtypeStruct((1, PRE, half), jnp.bfloat16),
            jax.ShapeDtypeStruct((1, PRE, half), jnp.bfloat16),
            jax.ShapeDtypeStruct(first.shape, jnp.float32),
        ),
        in_specs=[vmem] * 5,
        out_specs=[vmem] * 5,
        cost_estimate=pl.CostEstimate(flops=100_000, bytes_accessed=800_000, transcendentals=4_000),
        name="finish",
    )(kv_sum, owned, squares, first, second)


def swap(x, axis):
    return lax.all_to_all(x, axis, 0, 0, tiled=True)


def on_device(
    queries, resp_keys, response_values, rotated_prompt_keys, prompt_value_rows,
    attention_output_gradient, output_grad, advantages, lengths, tree_mask,
    adapter, first_moment, second_moment,
):
    n_resp = lax.axis_size("resp")
    n_fsdp = lax.axis_size("fsdp")
    place = lax.axis_index("resp").astype(jnp.int32).reshape(1)
    own_kv = pack(resp_keys, response_values, rotated_prompt_keys, prompt_value_rows)
    kv = lax.all_gather(own_kv, "resp", axis=0, tiled=True)
    gathered = swap(shards(adapter, n_fsdp), "fsdp")
    out_cot, low_t, low_in, qs, gs, gt, blocks, bias = prepare(
        place, lengths, tree_mask[0], advantages, gathered, queries[0], output_grad[0],
        attention_output_gradient[0],
    )
    out_t, turned, kv_grad = attend(blocks, bias, qs, gs, gt, kv, n_resp)
    kv_sum = lax.psum_scatter(kv_grad, "resp", scatter_dimension=0, tiled=True)
    arrived = swap(pieces(out_t, low_t, low_in, out_cot, n_fsdp), "fsdp")
    q_grad = turn(turned)
    arrived, q_grad = lax.optimization_barrier((arrived, q_grad))
    copies = group_sum(arrived, n_resp)
    owned, squares = norm(swap(copies, "resp"), n_fsdp)
    squares = swap(squares, "fsdp")
    key_sum, value_sum, prompt_key_sum, prompt_value_sum, update = finish(
        kv_sum, owned, squares, first_moment, second_moment
    )
    return (q_grad[None], key_sum, value_sum, prompt_key_sum, prompt_value_sum, update)


def solution(mesh):
    tokens = P("fsdp", "resp", None)
    columns = P(None, "fsdp")
    in_specs = (
        (tokens,) * 7
        + (P("fsdp", "resp"), P("fsdp", None), P("fsdp", None, None))
        + (columns,) * 3
    )
    out_specs = (tokens,) * 5 + (columns,)
    return jax.shard_map(
        on_device, mesh=mesh, in_specs=in_specs, out_specs=out_specs, check_vma=False
    )
```

```python
import functools

import jax
import jax.numpy as jnp
from jax import lax
from jax.experimental import pallas as pl
from jax.experimental.pallas import tpu as pltpu
from jax.sharding import PartitionSpec as P

HEAD = 128
Q_HEADS = 20
KV_HEADS = 4
MEMBERS = Q_HEADS // KV_HEADS
BLK = 64
JOIN = 4
TOK = 128
PRE = 16
RANK = 16
LANES = 128

adapter_scale = 2.0
max_norm = 1.0
beta_first = 0.9
beta_second = 0.999
first_fix = 0.9999734386011124
second_fix = 0.0952078516
adam_eps = 1e-08

SCALE = HEAD ** (-0.5)
LOG2E = 1.4426950408889634
HIDDEN = -1e30

NT = (((1,), (1,)), ((), ()))
NN = (((1,), (0,)), ((), ()))
TN = (((0,), (0,)), ((), ()))


def dot(a, b, dims):
    return lax.dot_general(a, b, dims, preferred_element_type=jnp.float32)


def token_column(place_ref, lengths_ref, adv_ref):
    own = lengths_ref[0, place_ref[0]]
    weight = adv_ref[0, 0] / own.astype(jnp.float32)
    pos = lax.broadcasted_iota(jnp.int32, (TOK, LANES), 0)
    return jnp.where(pos < own, weight, 0.0)[:, :1]


def rows_of(i, size):
    return pl.ds(pl.multiple_of(i * size, size), size)


def block_rows(b2):
    per = TOK // BLK
    return pl.ds(pl.multiple_of((b2 // per) * (TOK + PRE) + PRE + (b2 % per) * BLK, PRE), BLK)


def block_bias(b2, r, lengths_ref, tree_ref):
    per = TOK // BLK
    r2 = b2 // per
    key_pos = (b2 % per) * BLK + lax.broadcasted_iota(jnp.int32, (BLK, TOK), 0)
    query_pos = lax.broadcasted_iota(jnp.int32, (BLK, TOK), 1)
    bit = jnp.where(query_pos < BLK, tree_ref[per * r, b2], tree_ref[per * r + 1, b2])
    reach = jnp.where(r2 == r, query_pos, TOK)
    seen = (bit == 1) & (key_pos < lengths_ref[0, r2]) & (key_pos <= reach)
    return jnp.where(seen, 0.0, HIDDEN)


def prepare_kernel(
    place_ref, lengths_ref, tree_ref, adv_ref, parts_ref, q_ref, og_ref, ag_ref,
    out_cot_ref, low_t_ref, low_in_ref, qs_ref, gs_ref, gt_ref, list_ref, bias_ref,
    whole_ref,
):
    n, _, _ = parts_ref.shape
    width = whole_ref.shape[1] // n
    for i in range(n):
        whole_ref[:, i * width : (i + 1) * width] = parts_ref[i, :, :width].astype(jnp.float32)
    split = ag_ref.shape[1]
    weight = token_column(place_ref, lengths_ref, adv_ref)
    out_cot_ref[...] = (weight * og_ref[...].astype(jnp.float32)).astype(jnp.bfloat16)
    low_in_ref[...] = whole_ref[:, :split].astype(jnp.bfloat16)
    low_out = whole_ref[:, split:].astype(jnp.bfloat16)
    low_t = dot(low_out, out_cot_ref[...], NT).astype(jnp.bfloat16)
    low_t_ref[...] = low_t
    for i in range(Q_HEADS):
        part = slice(i * HEAD, (i + 1) * HEAD)
        rows = slice(i * TOK, (i + 1) * TOK)
        added = adapter_scale * dot(low_t, low_in_ref[:, part], TN)
        grad = (weight * ag_ref[:, part].astype(jnp.float32) + added).astype(jnp.bfloat16)
        gs_ref[rows, :] = grad
        gt_ref[:, rows] = jnp.transpose(grad.astype(jnp.float32)).astype(jnp.bfloat16)
        qs_ref[rows, :] = q_ref[:, part]

    r = place_ref[0]
    per = TOK // BLK
    n_blocks = tree_ref.shape[1]
    first = n_blocks // per * PRE // BLK
    bias_ref[: first * BLK, :] = jnp.zeros((first * BLK, TOK), jnp.float32)

    def step(b2, count):
        bits = tree_ref[per * r, b2] + tree_ref[per * r + 1, b2]
        seen = (bits > 0) & ((b2 % per) * BLK < lengths_ref[0, b2 // per])

        @pl.when(seen)
        def _():
            list_ref[2 + count - first] = b2
            bias_ref[rows_of(count, BLK), :] = block_bias(b2, r, lengths_ref, tree_ref)

        return count + jnp.where(seen, 1, 0)

    count = lax.fori_loop(0, n_blocks, step, first)
    steps = (count + JOIN - 1) // JOIN
    list_ref[0] = count
    list_ref[1] = steps

    def hide(i, carry):
        bias_ref[rows_of(i, BLK), :] = jnp.full((BLK, TOK), HIDDEN, jnp.float32)
        return carry

    lax.fori_loop(count, steps * JOIN, hide, 0)


def places_of(n_blocks):
    places = n_blocks + n_blocks // (TOK // BLK) * PRE // BLK
    return -(-places // JOIN) * JOIN


def prepare(place, lengths, tree, advantages, parts, q, og, ag):
    smem = pl.BlockSpec(memory_space=pltpu.SMEM)
    vmem = pl.BlockSpec(memory_space=pltpu.VMEM)
    split = ag.shape[1]
    wide = split + og.shape[1]
    n_blocks = tree.shape[1]
    return pl.pallas_call(
        prepare_kernel,
        out_shape=(
            jax.ShapeDtypeStruct(og.shape, jnp.bfloat16),
            jax.ShapeDtypeStruct((RANK, TOK), jnp.bfloat16),
            jax.ShapeDtypeStruct((RANK, split), jnp.bfloat16),
            jax.ShapeDtypeStruct((split, HEAD), jnp.bfloat16),
            jax.ShapeDtypeStruct((split, HEAD), jnp.bfloat16),
            jax.ShapeDtypeStruct((HEAD, split), jnp.bfloat16),
            jax.ShapeDtypeStruct((n_blocks + 2,), jnp.int32),
            jax.ShapeDtypeStruct((places_of(n_blocks) * BLK, TOK), jnp.float32),
        ),
        in_specs=[smem] * 4 + [vmem] * 4,
        out_specs=[vmem] * 6 + [smem, vmem],
        scratch_shapes=[pltpu.VMEM((RANK, wide), jnp.float32)],
        compiler_params=pltpu.CompilerParams(vmem_limit_bytes=16 * 1024 * 1024),
        cost_estimate=pl.CostEstimate(flops=80_000_000, bytes_accessed=6_000_000, transcendentals=0),
        name="prepare",
    )(place, lengths, tree, advantages, parts, q, og, ag)


def spread(bias):
    return jnp.concatenate([bias] * MEMBERS, axis=1)


def fold(x, op):
    return op(x.reshape(x.shape[0] // 8, 8, x.shape[1]), axis=0)


def attend_kernel(
    list_ref, bias_hbm, qs_hbm, gs_hbm, gt_hbm, low_t_hbm, low_in_hbm, out_cot_hbm, kv_ref,
    wide_out, turned_out, kv_grad_ref,
    bias_ref, qs_ref, gs_ref, gt_ref, low_t_ref, low_in_ref, out_cot_ref, keys_ref, score_ref, acc_ref,
    peak_ref, total_ref, inner_ref, wide_ref, turned_ref, sums_ref, zero_ref,
    in_sem, q_sem, bias_sem, place_sem, prompt_in_sem, prompt_sem, block_sem, wide_sem, turned_sem,
):
    c = SCALE * LOG2E
    n_blocks = block_sem.shape[0]
    n_resp = prompt_sem.shape[0]
    first = n_resp * PRE // BLK
    group = MEMBERS * TOK
    v0 = KV_HEADS * HEAD
    width = JOIN * BLK
    count = list_ref[0]
    steps = list_ref[1]

    def load(src, dst, i):
        return pltpu.make_async_copy(src, dst, in_sem.at[i])

    later = [
        load(src, dst, i)
        for i, (src, dst) in enumerate(
            (
                (gt_hbm, gt_ref),
                (low_t_hbm, low_t_ref),
                (low_in_hbm, low_in_ref),
                (out_cot_hbm, out_cot_ref),
                (gs_hbm, gs_ref),
            )
        )
    ]
    load_q = [
        pltpu.make_async_copy(
            qs_hbm.at[pl.ds(h * group, group)], qs_ref.at[pl.ds(h * group, group)], q_sem.at[h]
        )
        for h in range(KV_HEADS)
    ]

    def load_bias(i):
        return pltpu.make_async_copy(
            bias_hbm.at[rows_of(i, width)], bias_ref.at[rows_of(i, width)], bias_sem.at[i]
        )

    prompt_in = [
        pltpu.make_async_copy(
            kv_ref.at[pl.ds(i * (TOK + PRE), PRE)], keys_ref.at[pl.ds(i * PRE, PRE)], prompt_in_sem.at[i]
        )
        for i in range(n_resp)
    ]

    def bring(i):
        b2 = list_ref[2 + i - first]
        return pltpu.make_async_copy(kv_ref.at[block_rows(b2)], keys_ref.at[rows_of(i, BLK)], place_sem.at[i])

    def start(i, carry):
        bring(i).start()
        return carry

    def start_bias(i, carry):
        load_bias(i).start()
        return carry

    for copy in prompt_in:
        copy.start()
    load_q[0].start()
    lax.fori_loop(0, steps, start_bias, 0)
    lax.fori_loop(first, count, start, 0)
    for copy in load_q[1:]:
        copy.start()
    for copy in later:
        copy.start()

    zero_ref[...] = jnp.zeros_like(zero_ref)
    peak_ref[...] = jnp.full_like(peak_ref, HIDDEN)
    total_ref[...] = jnp.zeros_like(total_ref)
    acc_ref[...] = jnp.zeros_like(acc_ref)

    def blank(i, carry):
        keys_ref[rows_of(i, BLK), :] = jnp.zeros((BLK, keys_ref.shape[1]), jnp.bfloat16)
        return carry

    lax.fori_loop(count, steps * JOIN, blank, 0)

    def block_out(src, b2):
        return pltpu.make_async_copy(src, kv_grad_ref.at[block_rows(b2)], block_sem.at[b2])

    def unseen(b2, at):
        hit = (at < count) & (list_ref[jnp.minimum(2 + at - first, n_blocks + 1)] == b2)

        @pl.when(jnp.logical_not(hit))
        def _():
            block_out(zero_ref, b2).start()

        return at + jnp.where(hit, 1, 0)

    for copy in prompt_in:
        copy.wait()
    for copy in load_q:
        copy.wait()

    def cols(h):
        return slice(h * group, (h + 1) * group)

    def score_step(i, carry):
        def arrive(at, carry):
            bring(at).wait()
            return carry

        lax.fori_loop(jnp.maximum(i * JOIN, first), jnp.minimum((i + 1) * JOIN, count), arrive, 0)
        load_bias(i).wait()
        rows = rows_of(i, width)
        bias = spread(bias_ref[rows, :])
        for h in range(KV_HEADS):
            s = dot(keys_ref[rows, h * HEAD : (h + 1) * HEAD], qs_ref[cols(h), :], NT) + bias
            score_ref[rows, cols(h)] = s
            peak_ref[:, cols(h)] = jnp.maximum(peak_ref[:, cols(h)], fold(s, jnp.max))
        return carry

    lax.fori_loop(0, steps, score_step, 0)
    lax.fori_loop(0, n_blocks, unseen, first)
    peak = jnp.max(peak_ref[...], axis=0, keepdims=True) * c
    peak_ref[...] = jnp.broadcast_to(peak, peak_ref.shape)

    def value_step(i, carry):
        rows = rows_of(i, width)
        for h in range(KV_HEADS):
            e = jnp.exp2(score_ref[rows, cols(h)] * c - peak_ref[:1, cols(h)])
            score_ref[rows, cols(h)] = e
            total_ref[:, cols(h)] += fold(e, jnp.sum)
            v = keys_ref[rows, v0 + h * HEAD : v0 + (h + 1) * HEAD]
            acc_ref[:, cols(h)] += dot(v, e.astype(jnp.bfloat16), TN)
        return carry

    lax.fori_loop(0, steps, value_step, 0)
    inverse = 1.0 / jnp.sum(total_ref[...], axis=0, keepdims=True)
    total_ref[...] = jnp.broadcast_to(inverse, total_ref.shape)
    for copy in later:
        copy.wait()
    projected_t = jnp.zeros((RANK, TOK), jnp.float32)
    for i in range(Q_HEADS):
        part = slice(i * TOK, (i + 1) * TOK)
        rounded = (acc_ref[:, part] * inverse[:, part]).astype(jnp.bfloat16)
        projected_t += dot(low_in_ref[:, part], rounded, NN)
        wide_ref[:, part] = (adapter_scale * dot(low_t_ref[...], rounded, NT)).astype(jnp.bfloat16)
        across = gt_ref[:, part].astype(jnp.float32) * rounded.astype(jnp.float32)
        inner_ref[:, part] = jnp.broadcast_to(jnp.sum(across, axis=0, keepdims=True), (8, TOK))
    acc_ref[...] = jnp.zeros_like(acc_ref)
    split = acc_ref.shape[1]
    wide_ref[:, split:] = (
        adapter_scale * dot(projected_t.astype(jnp.bfloat16), out_cot_ref[...], NN)
    ).astype(jnp.bfloat16)
    send_wide = pltpu.make_async_copy(wide_ref, wide_out, wide_sem.at[0])
    send_wide.start()

    def back_step(i, carry):
        rows = rows_of(i, width)
        for h in range(KV_HEADS):
            kc = slice(h * HEAD, (h + 1) * HEAD)
            vc = slice(v0 + h * HEAD, v0 + (h + 1) * HEAD)
            w = score_ref[rows, cols(h)] * total_ref[:1, cols(h)]
            across = dot(keys_ref[rows, vc], gs_ref[cols(h), :], NT)
            sums_ref[rows, vc] = dot(w.astype(jnp.bfloat16), gs_ref[cols(h), :], NN).astype(jnp.bfloat16)
            ds = (w * (across - inner_ref[:1, cols(h)])).astype(jnp.bfloat16)
            sums_ref[rows, kc] = (dot(ds, qs_ref[cols(h), :], NN) * SCALE).astype(jnp.bfloat16)
            acc_ref[:, cols(h)] += dot(keys_ref[rows, kc], ds, TN)

        def send(at, carry):
            block_out(sums_ref.at[rows_of(at, BLK)], list_ref[2 + at - first]).start()
            return carry

        lax.fori_loop(jnp.maximum(i * JOIN, first), jnp.minimum((i + 1) * JOIN, count), send, 0)
        return carry

    lax.fori_loop(0, steps, back_step, 0)
    prompts = [
        pltpu.make_async_copy(
            sums_ref.at[pl.ds(i * PRE, PRE)], kv_grad_ref.at[pl.ds(i * (TOK + PRE), PRE)], prompt_sem.at[i]
        )
        for i in range(n_resp)
    ]
    for copy in prompts:
        copy.start()
    back = []
    for h in range(KV_HEADS):
        part = pl.ds(h * group, group)
        turned_ref[:, cols(h)] = (acc_ref[:, cols(h)] * SCALE).astype(jnp.bfloat16)
        back.append(pltpu.make_async_copy(turned_ref.at[:, part], turned_out.at[:, part], turned_sem.at[h]))
        back[-1].start()
    for copy in prompts + back + [send_wide]:
        copy.wait()

    def finished(b2, carry):
        block_out(zero_ref, b2).wait()
        return carry

    lax.fori_loop(0, n_blocks, finished, 0)


def attend(blocks, bias, qs, gs, gt, low_t, low_in, out_cot, kv, n_resp):
    smem = pl.BlockSpec(memory_space=pltpu.SMEM)
    hbm = pl.BlockSpec(memory_space=pl.ANY)
    split = qs.shape[0]
    wide = split + out_cot.shape[1]
    rows, columns = bias.shape[0], kv.shape[1]
    return pl.pallas_call(
        attend_kernel,
        out_shape=(
            jax.ShapeDtypeStruct((RANK, wide), jnp.bfloat16),
            jax.ShapeDtypeStruct((HEAD, split), jnp.bfloat16),
            jax.ShapeDtypeStruct(kv.shape, jnp.bfloat16),
        ),
        in_specs=[smem] + [hbm] * 8,
        out_specs=[hbm] * 3,
        scratch_shapes=[
            pltpu.VMEM(bias.shape, jnp.float32),
            pltpu.VMEM(qs.shape, jnp.bfloat16),
            pltpu.VMEM(gs.shape, jnp.bfloat16),
            pltpu.VMEM(gt.shape, jnp.bfloat16),
            pltpu.VMEM(low_t.shape, jnp.bfloat16),
            pltpu.VMEM(low_in.shape, jnp.bfloat16),
            pltpu.VMEM(out_cot.shape, jnp.bfloat16),
            pltpu.VMEM((rows, columns), jnp.bfloat16),
            pltpu.VMEM((rows, split), jnp.float32),
            pltpu.VMEM((HEAD, split), jnp.float32),
            pltpu.VMEM((8, split), jnp.float32),
            pltpu.VMEM((8, split), jnp.float32),
            pltpu.VMEM((8, split), jnp.float32),
            pltpu.VMEM((RANK, wide), jnp.bfloat16),
            pltpu.VMEM((HEAD, split), jnp.bfloat16),
            pltpu.VMEM((rows, columns), jnp.bfloat16),
            pltpu.VMEM((BLK, columns), jnp.bfloat16),
            pltpu.SemaphoreType.DMA((5,)),
            pltpu.SemaphoreType.DMA((KV_HEADS,)),
            pltpu.SemaphoreType.DMA((rows // (JOIN * BLK),)),
            pltpu.SemaphoreType.DMA((rows // BLK,)),
            pltpu.SemaphoreType.DMA((n_resp,)),
            pltpu.SemaphoreType.DMA((n_resp,)),
            pltpu.SemaphoreType.DMA((n_resp * (TOK // BLK),)),
            pltpu.SemaphoreType.DMA((1,)),
            pltpu.SemaphoreType.DMA((KV_HEADS,)),
        ],
        compiler_params=pltpu.CompilerParams(vmem_limit_bytes=56 * 1024 * 1024),
        cost_estimate=pl.CostEstimate(
            flops=3_800_000_000, bytes_accessed=8_000_000, transcendentals=3_000_000
        ),
        name="attend",
    )(blocks, bias, qs, gs, gt, low_t, low_in, out_cot, kv)


def pieces_kernel(wide_ref, parts_ref, whole_ref):
    whole_ref[...] = wide_ref[...].astype(jnp.float32)
    n_parts = parts_ref.shape[0]
    piece = whole_ref.shape[1] // n_parts
    fill = jnp.zeros((RANK, LANES - piece), jnp.float32)
    for i in range(n_parts):
        part = whole_ref[:, i * piece : (i + 1) * piece]
        parts_ref[i] = jnp.concatenate([part, fill], axis=1).astype(jnp.bfloat16)


PIECES_FLOPS = 200_000_000_000


def pieces(wide, n_fsdp):
    vmem = pl.BlockSpec(memory_space=pltpu.VMEM)
    return pl.pallas_call(
        pieces_kernel,
        out_shape=jax.ShapeDtypeStruct((n_fsdp, RANK, LANES), jnp.bfloat16),
        in_specs=[vmem],
        out_specs=vmem,
        scratch_shapes=[pltpu.VMEM(wide.shape, jnp.float32)],
        cost_estimate=pl.CostEstimate(flops=PIECES_FLOPS, bytes_accessed=500_000, transcendentals=0),
        name="pieces",
    )(wide)


def turn_kernel(turned_ref, out_ref):
    for i in range(Q_HEADS):
        part = slice(i * TOK, (i + 1) * TOK)
        out_ref[:, part] = jnp.transpose(turned_ref[:, part].astype(jnp.float32)).astype(jnp.bfloat16)


def turn(turned):
    vmem = pl.BlockSpec(memory_space=pltpu.VMEM)
    return pl.pallas_call(
        turn_kernel,
        out_shape=jax.ShapeDtypeStruct((TOK, turned.shape[1]), jnp.bfloat16),
        in_specs=[vmem],
        out_specs=vmem,
        cost_estimate=pl.CostEstimate(flops=1_000_000, bytes_accessed=1_300_000, transcendentals=0),
        name="turn",
    )(turned)


def pack_kernel(rk_ref, rv_ref, pk_ref, pv_ref, own_ref):
    half = rk_ref.shape[2]
    own_ref[:PRE, :half] = pk_ref[0]
    own_ref[:PRE, half:] = pv_ref[0]
    own_ref[PRE:, :half] = rk_ref[0]
    own_ref[PRE:, half:] = rv_ref[0]


def pack(rk, rv, pk, pv):
    vmem = pl.BlockSpec(memory_space=pltpu.VMEM)
    return pl.pallas_call(
        pack_kernel,
        out_shape=jax.ShapeDtypeStruct((PRE + rk.shape[1], 2 * rk.shape[2]), jnp.bfloat16),
        in_specs=[vmem] * 4,
        out_specs=vmem,
        cost_estimate=pl.CostEstimate(flops=1_000, bytes_accessed=600_000, transcendentals=0),
        name="pack",
    )(rk, rv, pk, pv)


def shards_kernel(adapter_ref, parts_ref):
    width = adapter_ref.shape[1]
    parts_ref[0] = jnp.zeros(parts_ref.shape[1:], jnp.bfloat16)
    parts_ref[0, :, :width] = adapter_ref[...].astype(jnp.bfloat16)
    shard = parts_ref[0]
    for i in range(1, parts_ref.shape[0]):
        parts_ref[i] = shard


def shards(adapter, n_fsdp):
    vmem = pl.BlockSpec(memory_space=pltpu.VMEM)
    return pl.pallas_call(
        shards_kernel,
        out_shape=jax.ShapeDtypeStruct((n_fsdp, RANK, LANES), jnp.bfloat16),
        in_specs=[vmem],
        out_specs=vmem,
        cost_estimate=pl.CostEstimate(flops=1_000, bytes_accessed=300_000, transcendentals=0),
        name="shards",
    )(adapter)


def unpack_kernel(kv_ref, rk_ref, rv_ref, pk_ref, pv_ref):
    half = rk_ref.shape[2]
    rk_ref[0] = kv_ref[PRE:, :half]
    rv_ref[0] = kv_ref[PRE:, half:]
    pk_ref[0] = kv_ref[:PRE, :half]
    pv_ref[0] = kv_ref[:PRE, half:]


def unpack(kv_sum):
    vmem = pl.BlockSpec(memory_space=pltpu.VMEM)
    half = kv_sum.shape[1] // 2
    return pl.pallas_call(
        unpack_kernel,
        out_shape=(
            jax.ShapeDtypeStruct((1, TOK, half), jnp.bfloat16),
            jax.ShapeDtypeStruct((1, TOK, half), jnp.bfloat16),
            jax.ShapeDtypeStruct((1, PRE, half), jnp.bfloat16),
            jax.ShapeDtypeStruct((1, PRE, half), jnp.bfloat16),
        ),
        in_specs=[vmem],
        out_specs=[vmem] * 4,
        cost_estimate=pl.CostEstimate(flops=1_000, bytes_accessed=600_000, transcendentals=0),
        name="unpack",
    )(kv_sum)


def adam_update_of(gradient, first_state, second_state, clip_factor):
    scaled = gradient * clip_factor
    moment = beta_first * first_state + (1.0 - beta_first) * scaled
    second_new = beta_second * second_state + (1.0 - beta_second) * scaled * scaled
    return moment / first_fix / (jnp.sqrt(second_new / second_fix) + adam_eps)


def swap(x, axis):
    return lax.all_to_all(x, axis, 0, 0, tiled=True)


def on_device(
    queries, resp_keys, response_values, rotated_prompt_keys, prompt_value_rows,
    attention_output_gradient, output_grad, advantages, lengths, tree_mask,
    adapter, first_moment, second_moment,
):
    n_resp = lax.axis_size("resp")
    n_fsdp = lax.axis_size("fsdp")
    place = lax.axis_index("resp").astype(jnp.int32).reshape(1)
    own_kv = pack(resp_keys, response_values, rotated_prompt_keys, prompt_value_rows)
    kv = lax.all_gather(own_kv, "resp", axis=0, tiled=True)
    gathered = swap(shards(adapter, n_fsdp), "fsdp")
    out_cot, low_t, low_in, qs, gs, gt, blocks, bias = prepare(
        place, lengths, tree_mask[0], advantages, gathered, queries[0], output_grad[0],
        attention_output_gradient[0],
    )
    wide, turned, kv_grad = attend(blocks, bias, qs, gs, gt, low_t, low_in, out_cot, kv, n_resp)
    kv_sum = lax.psum_scatter(kv_grad, "resp", scatter_dimension=0, tiled=True)
    arrived = swap(pieces(wide, n_fsdp), "fsdp")
    q_grad = turn(turned)
    arrived, q_grad = lax.optimization_barrier((arrived, q_grad))
    group = jnp.sum(arrived.astype(jnp.float32), axis=0)
    owned = jnp.sum(swap(jnp.broadcast_to(group, (n_resp,) + group.shape), "resp"), axis=0)
    squares = jnp.broadcast_to(jnp.sum(owned * owned), (n_fsdp, 1, LANES))
    squares = swap(squares, "fsdp")
    sums = unpack(kv_sum)
    squares, sums = lax.optimization_barrier((squares, sums))
    clip_factor = max_norm / jnp.maximum(jnp.sqrt(jnp.sum(squares[:, 0, 0])), max_norm)
    update = adam_update_of(owned[:, : adapter.shape[1]], first_moment, second_moment, clip_factor)
    return (q_grad[None],) + tuple(sums) + (update,)


def solution(mesh):
    tokens = P("fsdp", "resp", None)
    columns = P(None, "fsdp")
    in_specs = (
        (tokens,) * 7
        + (P("fsdp", "resp"), P("fsdp", None), P("fsdp", None, None))
        + (columns,) * 3
    )
    out_specs = (tokens,) * 5 + (columns,)
    return jax.shard_map(
        on_device, mesh=mesh, in_specs=in_specs, out_specs=out_specs, check_vma=False
    )
```

```python
import functools

import jax
import jax.numpy as jnp
from jax import lax
from jax.experimental import pallas as pl
from jax.experimental.pallas import tpu as pltpu
from jax.sharding import PartitionSpec as P

HEAD = 128
Q_HEADS = 20
KV_HEADS = 4
MEMBERS = Q_HEADS // KV_HEADS
BLK = 64
JOIN = 4
TOK = 128
PRE = 16
RANK = 16
LANES = 128

adapter_scale = 2.0
max_norm = 1.0
beta_first = 0.9
beta_second = 0.999
first_fix = 0.9999734386011124
second_fix = 0.0952078516
adam_eps = 1e-08

SCALE = HEAD ** (-0.5)
LOG2E = 1.4426950408889634
HIDDEN = -1e30

NT = (((1,), (1,)), ((), ()))
NN = (((1,), (0,)), ((), ()))
TN = (((0,), (0,)), ((), ()))


def dot(a, b, dims):
    return lax.dot_general(a, b, dims, preferred_element_type=jnp.float32)


def token_column(place_ref, lengths_ref, adv_ref):
    own = lengths_ref[0, place_ref[0]]
    weight = adv_ref[0, 0] / own.astype(jnp.float32)
    pos = lax.broadcasted_iota(jnp.int32, (TOK, LANES), 0)
    return jnp.where(pos < own, weight, 0.0)[:, :1]


def rows_of(i, size):
    return pl.ds(pl.multiple_of(i * size, size), size)


def block_rows(b2):
    per = TOK // BLK
    return pl.ds(pl.multiple_of((b2 // per) * (TOK + PRE) + PRE + (b2 % per) * BLK, PRE), BLK)


def block_bias(b2, r, lengths_ref, tree_ref):
    per = TOK // BLK
    r2 = b2 // per
    key_pos = (b2 % per) * BLK + lax.broadcasted_iota(jnp.int32, (BLK, TOK), 0)
    query_pos = lax.broadcasted_iota(jnp.int32, (BLK, TOK), 1)
    bit = jnp.where(query_pos < BLK, tree_ref[per * r, b2], tree_ref[per * r + 1, b2])
    reach = jnp.where(r2 == r, query_pos, TOK)
    seen = (bit == 1) & (key_pos < lengths_ref[0, r2]) & (key_pos <= reach)
    return jnp.where(seen, 0.0, HIDDEN)


def prepare_kernel(
    place_ref, lengths_ref, tree_ref, adv_ref, parts_ref, q_ref, og_ref, ag_ref,
    out_cot_ref, low_t_ref, low_in_ref, qs_ref, gs_ref, gt_ref, list_ref, bias_ref,
    whole_ref,
):
    n, _, _ = parts_ref.shape
    width = whole_ref.shape[1] // n
    for i in range(n):
        whole_ref[:, i * width : (i + 1) * width] = parts_ref[i, :, :width].astype(jnp.float32)
    split = ag_ref.shape[1]
    weight = token_column(place_ref, lengths_ref, adv_ref)
    out_cot_ref[...] = (weight * og_ref[...].astype(jnp.float32)).astype(jnp.bfloat16)
    low_in_ref[...] = whole_ref[:, :split].astype(jnp.bfloat16)
    low_out = whole_ref[:, split:].astype(jnp.bfloat16)
    low_t = dot(low_out, out_cot_ref[...], NT).astype(jnp.bfloat16)
    low_t_ref[...] = low_t
    for i in range(Q_HEADS):
        part = slice(i * HEAD, (i + 1) * HEAD)
        rows = slice(i * TOK, (i + 1) * TOK)
        added = adapter_scale * dot(low_t, low_in_ref[:, part], TN)
        grad = (weight * ag_ref[:, part].astype(jnp.float32) + added).astype(jnp.bfloat16)
        gs_ref[rows, :] = grad
        gt_ref[:, rows] = jnp.transpose(grad.astype(jnp.float32)).astype(jnp.bfloat16)
        qs_ref[rows, :] = q_ref[:, part]

    r = place_ref[0]
    per = TOK // BLK
    n_blocks = tree_ref.shape[1]
    first = n_blocks // per * PRE // BLK
    bias_ref[: first * BLK, :] = jnp.zeros((first * BLK, TOK), jnp.float32)

    def step(b2, count):
        bits = tree_ref[per * r, b2] + tree_ref[per * r + 1, b2]
        seen = (bits > 0) & ((b2 % per) * BLK < lengths_ref[0, b2 // per])

        @pl.when(seen)
        def _():
            list_ref[2 + count - first] = b2
            bias_ref[rows_of(count, BLK), :] = block_bias(b2, r, lengths_ref, tree_ref)

        return count + jnp.where(seen, 1, 0)

    count = lax.fori_loop(0, n_blocks, step, first)
    steps = (count + JOIN - 1) // JOIN
    list_ref[0] = count
    list_ref[1] = steps

    def hide(i, carry):
        bias_ref[rows_of(i, BLK), :] = jnp.full((BLK, TOK), HIDDEN, jnp.float32)
        return carry

    lax.fori_loop(count, steps * JOIN, hide, 0)


def places_of(n_blocks):
    places = n_blocks + n_blocks // (TOK // BLK) * PRE // BLK
    return -(-places // JOIN) * JOIN


def prepare(place, lengths, tree, advantages, parts, q, og, ag):
    smem = pl.BlockSpec(memory_space=pltpu.SMEM)
    vmem = pl.BlockSpec(memory_space=pltpu.VMEM)
    split = ag.shape[1]
    wide = split + og.shape[1]
    n_blocks = tree.shape[1]
    return pl.pallas_call(
        prepare_kernel,
        out_shape=(
            jax.ShapeDtypeStruct(og.shape, jnp.bfloat16),
            jax.ShapeDtypeStruct((RANK, TOK), jnp.bfloat16),
            jax.ShapeDtypeStruct((RANK, split), jnp.bfloat16),
            jax.ShapeDtypeStruct((split, HEAD), jnp.bfloat16),
            jax.ShapeDtypeStruct((split, HEAD), jnp.bfloat16),
            jax.ShapeDtypeStruct((HEAD, split), jnp.bfloat16),
            jax.ShapeDtypeStruct((n_blocks + 2,), jnp.int32),
            jax.ShapeDtypeStruct((places_of(n_blocks) * BLK, TOK), jnp.float32),
        ),
        in_specs=[smem] * 4 + [vmem] * 4,
        out_specs=[vmem] * 6 + [smem, vmem],
        scratch_shapes=[pltpu.VMEM((RANK, wide), jnp.float32)],
        compiler_params=pltpu.CompilerParams(vmem_limit_bytes=16 * 1024 * 1024),
        cost_estimate=pl.CostEstimate(flops=80_000_000, bytes_accessed=6_000_000, transcendentals=0),
        name="prepare",
    )(place, lengths, tree, advantages, parts, q, og, ag)


def spread(bias):
    return jnp.concatenate([bias] * MEMBERS, axis=1)


def fold(x, op):
    return op(x.reshape(x.shape[0] // 8, 8, x.shape[1]), axis=0)


def attend_kernel(
    list_ref, bias_hbm, qs_hbm, gs_hbm, gt_hbm, low_t_hbm, low_in_hbm, out_cot_hbm, kv_ref,
    parts_out, turned_out, kv_grad_ref,
    bias_ref, qs_ref, gs_ref, gt_ref, low_t_ref, low_in_ref, out_cot_ref, keys_ref, score_ref, acc_ref,
    peak_ref, total_ref, inner_ref, wide_ref, parts_ref, turned_ref, sums_ref, zero_ref,
    in_sem, q_sem, bias_sem, place_sem, prompt_in_sem, prompt_sem, block_sem, wide_sem, turned_sem,
):
    c = SCALE * LOG2E
    n_blocks = block_sem.shape[0]
    n_resp = prompt_sem.shape[0]
    first = n_resp * PRE // BLK
    group = MEMBERS * TOK
    v0 = KV_HEADS * HEAD
    width = JOIN * BLK
    count = list_ref[0]
    steps = list_ref[1]

    def load(src, dst, i):
        return pltpu.make_async_copy(src, dst, in_sem.at[i])

    later = [
        load(src, dst, i)
        for i, (src, dst) in enumerate(
            (
                (gt_hbm, gt_ref),
                (low_t_hbm, low_t_ref),
                (low_in_hbm, low_in_ref),
                (out_cot_hbm, out_cot_ref),
                (gs_hbm, gs_ref),
            )
        )
    ]
    load_q = [
        pltpu.make_async_copy(
            qs_hbm.at[pl.ds(h * group, group)], qs_ref.at[pl.ds(h * group, group)], q_sem.at[h]
        )
        for h in range(KV_HEADS)
    ]

    def load_bias(i):
        return pltpu.make_async_copy(
            bias_hbm.at[rows_of(i, width)], bias_ref.at[rows_of(i, width)], bias_sem.at[i]
        )

    prompt_in = [
        pltpu.make_async_copy(
            kv_ref.at[pl.ds(i * (TOK + PRE), PRE)], keys_ref.at[pl.ds(i * PRE, PRE)], prompt_in_sem.at[i]
        )
        for i in range(n_resp)
    ]

    def bring(i):
        b2 = list_ref[2 + i - first]
        return pltpu.make_async_copy(kv_ref.at[block_rows(b2)], keys_ref.at[rows_of(i, BLK)], place_sem.at[i])

    def start(i, carry):
        bring(i).start()
        return carry

    def start_bias(i, carry):
        load_bias(i).start()
        return carry

    for copy in prompt_in:
        copy.start()
    for copy in load_q:
        copy.start()
    lax.fori_loop(0, steps, start_bias, 0)
    lax.fori_loop(first, count, start, 0)
    for copy in later:
        copy.start()

    zero_ref[...] = jnp.zeros_like(zero_ref)
    peak_ref[...] = jnp.full_like(peak_ref, HIDDEN)
    total_ref[...] = jnp.zeros_like(total_ref)
    acc_ref[...] = jnp.zeros_like(acc_ref)

    def blank(i, carry):
        keys_ref[rows_of(i, BLK), :] = jnp.zeros((BLK, keys_ref.shape[1]), jnp.bfloat16)
        return carry

    lax.fori_loop(count, steps * JOIN, blank, 0)

    def block_out(src, b2):
        return pltpu.make_async_copy(src, kv_grad_ref.at[block_rows(b2)], block_sem.at[b2])

    def unseen(b2, at):
        hit = (at < count) & (list_ref[jnp.minimum(2 + at - first, n_blocks + 1)] == b2)

        @pl.when(jnp.logical_not(hit))
        def _():
            block_out(zero_ref, b2).start()

        return at + jnp.where(hit, 1, 0)

    for copy in prompt_in:
        copy.wait()
    for copy in load_q:
        copy.wait()

    def cols(h):
        return slice(h * group, (h + 1) * group)

    def score_step(i, carry):
        def arrive(at, carry):
            bring(at).wait()
            return carry

        lax.fori_loop(jnp.maximum(i * JOIN, first), jnp.minimum((i + 1) * JOIN, count), arrive, 0)
        load_bias(i).wait()
        rows = rows_of(i, width)
        bias = spread(bias_ref[rows, :])
        for h in range(KV_HEADS):
            s = dot(keys_ref[rows, h * HEAD : (h + 1) * HEAD], qs_ref[cols(h), :], NT) + bias
            score_ref[rows, cols(h)] = s
            peak_ref[:, cols(h)] = jnp.maximum(peak_ref[:, cols(h)], fold(s, jnp.max))
        return carry

    lax.fori_loop(0, steps, score_step, 0)
    peak = jnp.max(peak_ref[...], axis=0, keepdims=True) * c
    peak_ref[...] = jnp.broadcast_to(peak, peak_ref.shape)

    def value_step(i, carry):
        rows = rows_of(i, width)
        for h in range(KV_HEADS):
            e = jnp.exp2(score_ref[rows, cols(h)] * c - peak_ref[:1, cols(h)])
            score_ref[rows, cols(h)] = e
            total_ref[:, cols(h)] += fold(e, jnp.sum)
            v = keys_ref[rows, v0 + h * HEAD : v0 + (h + 1) * HEAD]
            acc_ref[:, cols(h)] += dot(v, e.astype(jnp.bfloat16), TN)
        return carry

    lax.fori_loop(0, steps, value_step, 0)
    lax.fori_loop(0, n_blocks, unseen, first)
    inverse = 1.0 / jnp.sum(total_ref[...], axis=0, keepdims=True)
    total_ref[...] = jnp.broadcast_to(inverse, total_ref.shape)
    for copy in later:
        copy.wait()
    projected_t = jnp.zeros((RANK, TOK), jnp.float32)
    for i in range(Q_HEADS):
        part = slice(i * TOK, (i + 1) * TOK)
        rounded = (acc_ref[:, part] * inverse[:, part]).astype(jnp.bfloat16)
        projected_t += dot(low_in_ref[:, part], rounded, NN)
        wide_ref[:, part] = adapter_scale * dot(low_t_ref[...], rounded, NT)
        across = gt_ref[:, part].astype(jnp.float32) * rounded.astype(jnp.float32)
        inner_ref[:, part] = jnp.broadcast_to(jnp.sum(across, axis=0, keepdims=True), (8, TOK))
    acc_ref[...] = jnp.zeros_like(acc_ref)
    split = acc_ref.shape[1]
    wide_ref[:, split:] = adapter_scale * dot(projected_t.astype(jnp.bfloat16), out_cot_ref[...], NN)
    n_parts = parts_ref.shape[0]
    piece = wide_ref.shape[1] // n_parts
    fill = jnp.zeros((RANK, LANES - piece), jnp.float32)
    for i in range(n_parts):
        part = wide_ref[:, i * piece : (i + 1) * piece]
        parts_ref[i] = jnp.concatenate([part, fill], axis=1).astype(jnp.bfloat16)
    send_parts = pltpu.make_async_copy(parts_ref, parts_out, wide_sem.at[0])
    send_parts.start()

    def back_step(i, carry):
        rows = rows_of(i, width)
        for h in range(KV_HEADS):
            kc = slice(h * HEAD, (h + 1) * HEAD)
            vc = slice(v0 + h * HEAD, v0 + (h + 1) * HEAD)
            w = score_ref[rows, cols(h)] * total_ref[:1, cols(h)]
            across = dot(keys_ref[rows, vc], gs_ref[cols(h), :], NT)
            sums_ref[rows, vc] = dot(w.astype(jnp.bfloat16), gs_ref[cols(h), :], NN).astype(jnp.bfloat16)
            ds = (w * (across - inner_ref[:1, cols(h)])).astype(jnp.bfloat16)
            sums_ref[rows, kc] = (dot(ds, qs_ref[cols(h), :], NN) * SCALE).astype(jnp.bfloat16)
            acc_ref[:, cols(h)] += dot(keys_ref[rows, kc], ds, TN)

        def send(at, carry):
            block_out(sums_ref.at[rows_of(at, BLK)], list_ref[2 + at - first]).start()
            return carry

        lax.fori_loop(jnp.maximum(i * JOIN, first), jnp.minimum((i + 1) * JOIN, count), send, 0)
        return carry

    lax.fori_loop(0, steps, back_step, 0)
    prompts = [
        pltpu.make_async_copy(
            sums_ref.at[pl.ds(i * PRE, PRE)], kv_grad_ref.at[pl.ds(i * (TOK + PRE), PRE)], prompt_sem.at[i]
        )
        for i in range(n_resp)
    ]
    for copy in prompts:
        copy.start()
    back = []
    for h in range(KV_HEADS):
        part = pl.ds(h * group, group)
        turned_ref[:, cols(h)] = (acc_ref[:, cols(h)] * SCALE).astype(jnp.bfloat16)
        back.append(pltpu.make_async_copy(turned_ref.at[:, part], turned_out.at[:, part], turned_sem.at[h]))
        back[-1].start()
    for copy in prompts + back + [send_parts]:
        copy.wait()

    def finished(b2, carry):
        block_out(zero_ref, b2).wait()
        return carry

    lax.fori_loop(0, n_blocks, finished, 0)


def attend(blocks, bias, qs, gs, gt, low_t, low_in, out_cot, kv, n_fsdp, n_resp):
    smem = pl.BlockSpec(memory_space=pltpu.SMEM)
    hbm = pl.BlockSpec(memory_space=pl.ANY)
    split = qs.shape[0]
    wide = split + out_cot.shape[1]
    rows, columns = bias.shape[0], kv.shape[1]
    return pl.pallas_call(
        attend_kernel,
        out_shape=(
            jax.ShapeDtypeStruct((n_fsdp, RANK, LANES), jnp.bfloat16),
            jax.ShapeDtypeStruct((HEAD, split), jnp.bfloat16),
            jax.ShapeDtypeStruct(kv.shape, jnp.bfloat16),
        ),
        in_specs=[smem] + [hbm] * 8,
        out_specs=[hbm] * 3,
        scratch_shapes=[
            pltpu.VMEM(bias.shape, jnp.float32),
            pltpu.VMEM(qs.shape, jnp.bfloat16),
            pltpu.VMEM(gs.shape, jnp.bfloat16),
            pltpu.VMEM(gt.shape, jnp.bfloat16),
            pltpu.VMEM(low_t.shape, jnp.bfloat16),
            pltpu.VMEM(low_in.shape, jnp.bfloat16),
            pltpu.VMEM(out_cot.shape, jnp.bfloat16),
            pltpu.VMEM((rows, columns), jnp.bfloat16),
            pltpu.VMEM((rows, split), jnp.float32),
            pltpu.VMEM((HEAD, split), jnp.float32),
            pltpu.VMEM((8, split), jnp.float32),
            pltpu.VMEM((8, split), jnp.float32),
            pltpu.VMEM((8, split), jnp.float32),
            pltpu.VMEM((RANK, wide), jnp.float32),
            pltpu.VMEM((n_fsdp, RANK, LANES), jnp.bfloat16),
            pltpu.VMEM((HEAD, split), jnp.bfloat16),
            pltpu.VMEM((rows, columns), jnp.bfloat16),
            pltpu.VMEM((BLK, columns), jnp.bfloat16),
            pltpu.SemaphoreType.DMA((5,)),
            pltpu.SemaphoreType.DMA((KV_HEADS,)),
            pltpu.SemaphoreType.DMA((rows // (JOIN * BLK),)),
            pltpu.SemaphoreType.DMA((rows // BLK,)),
            pltpu.SemaphoreType.DMA((n_resp,)),
            pltpu.SemaphoreType.DMA((n_resp,)),
            pltpu.SemaphoreType.DMA((n_resp * (TOK // BLK),)),
            pltpu.SemaphoreType.DMA((1,)),
            pltpu.SemaphoreType.DMA((KV_HEADS,)),
        ],
        compiler_params=pltpu.CompilerParams(vmem_limit_bytes=56 * 1024 * 1024),
        cost_estimate=pl.CostEstimate(
            flops=3_800_000_000, bytes_accessed=8_000_000, transcendentals=3_000_000
        ),
        name="attend",
    )(blocks, bias, qs, gs, gt, low_t, low_in, out_cot, kv)


def hold_kernel(parts_ref, same_ref):
    del parts_ref, same_ref


HOLD_FLOPS = 200_000_000_000


def hold(parts):
    hbm = pl.BlockSpec(memory_space=pl.ANY)
    return pl.pallas_call(
        hold_kernel,
        out_shape=jax.ShapeDtypeStruct(parts.shape, parts.dtype),
        in_specs=[hbm],
        out_specs=hbm,
        input_output_aliases={0: 0},
        cost_estimate=pl.CostEstimate(flops=HOLD_FLOPS, bytes_accessed=500_000, transcendentals=0),
        name="hold",
    )(parts)


def turn_kernel(turned_ref, out_ref):
    for i in range(Q_HEADS):
        part = slice(i * TOK, (i + 1) * TOK)
        out_ref[:, part] = jnp.transpose(turned_ref[:, part].astype(jnp.float32)).astype(jnp.bfloat16)


def turn(turned):
    vmem = pl.BlockSpec(memory_space=pltpu.VMEM)
    return pl.pallas_call(
        turn_kernel,
        out_shape=jax.ShapeDtypeStruct((TOK, turned.shape[1]), jnp.bfloat16),
        in_specs=[vmem],
        out_specs=vmem,
        cost_estimate=pl.CostEstimate(flops=1_000_000, bytes_accessed=1_300_000, transcendentals=0),
        name="turn",
    )(turned)


def pack_kernel(rk_ref, rv_ref, pk_ref, pv_ref, own_ref):
    half = rk_ref.shape[2]
    own_ref[:PRE, :half] = pk_ref[0]
    own_ref[:PRE, half:] = pv_ref[0]
    own_ref[PRE:, :half] = rk_ref[0]
    own_ref[PRE:, half:] = rv_ref[0]


def pack(rk, rv, pk, pv):
    vmem = pl.BlockSpec(memory_space=pltpu.VMEM)
    return pl.pallas_call(
        pack_kernel,
        out_shape=jax.ShapeDtypeStruct((PRE + rk.shape[1], 2 * rk.shape[2]), jnp.bfloat16),
        in_specs=[vmem] * 4,
        out_specs=vmem,
        cost_estimate=pl.CostEstimate(flops=1_000, bytes_accessed=600_000, transcendentals=0),
        name="pack",
    )(rk, rv, pk, pv)


def shards_kernel(adapter_ref, parts_ref):
    width = adapter_ref.shape[1]
    parts_ref[0] = jnp.zeros(parts_ref.shape[1:], jnp.bfloat16)
    parts_ref[0, :, :width] = adapter_ref[...].astype(jnp.bfloat16)
    shard = parts_ref[0]
    for i in range(1, parts_ref.shape[0]):
        parts_ref[i] = shard


def shards(adapter, n_fsdp):
    vmem = pl.BlockSpec(memory_space=pltpu.VMEM)
    return pl.pallas_call(
        shards_kernel,
        out_shape=jax.ShapeDtypeStruct((n_fsdp, RANK, LANES), jnp.bfloat16),
        in_specs=[vmem],
        out_specs=vmem,
        cost_estimate=pl.CostEstimate(flops=1_000, bytes_accessed=300_000, transcendentals=0),
        name="shards",
    )(adapter)


def unpack_kernel(kv_ref, rk_ref, rv_ref, pk_ref, pv_ref):
    half = rk_ref.shape[2]
    rk_ref[0] = kv_ref[PRE:, :half]
    rv_ref[0] = kv_ref[PRE:, half:]
    pk_ref[0] = kv_ref[:PRE, :half]
    pv_ref[0] = kv_ref[:PRE, half:]


def unpack(kv_sum):
    vmem = pl.BlockSpec(memory_space=pltpu.VMEM)
    half = kv_sum.shape[1] // 2
    return pl.pallas_call(
        unpack_kernel,
        out_shape=(
            jax.ShapeDtypeStruct((1, TOK, half), jnp.bfloat16),
            jax.ShapeDtypeStruct((1, TOK, half), jnp.bfloat16),
            jax.ShapeDtypeStruct((1, PRE, half), jnp.bfloat16),
            jax.ShapeDtypeStruct((1, PRE, half), jnp.bfloat16),
        ),
        in_specs=[vmem],
        out_specs=[vmem] * 4,
        cost_estimate=pl.CostEstimate(flops=1_000, bytes_accessed=600_000, transcendentals=0),
        name="unpack",
    )(kv_sum)


def adam_update_of(gradient, first_term, second_term, clip_factor):
    scaled = gradient * clip_factor
    moment = first_term + (1.0 - beta_first) * scaled
    second_new = second_term + (1.0 - beta_second) * scaled * scaled
    return moment / first_fix / (jnp.sqrt(second_new / second_fix) + adam_eps)


def swap(x, axis):
    return lax.all_to_all(x, axis, 0, 0, tiled=True)


def on_device(
    queries, resp_keys, response_values, rotated_prompt_keys, prompt_value_rows,
    attention_output_gradient, output_grad, advantages, lengths, tree_mask,
    adapter, first_moment, second_moment,
):
    n_resp = lax.axis_size("resp")
    n_fsdp = lax.axis_size("fsdp")
    place = lax.axis_index("resp").astype(jnp.int32).reshape(1)
    own_kv = pack(resp_keys, response_values, rotated_prompt_keys, prompt_value_rows)
    kv = lax.all_gather(own_kv, "resp", axis=0, tiled=True)
    gathered = swap(shards(adapter, n_fsdp), "fsdp")
    out_cot, low_t, low_in, qs, gs, gt, blocks, bias = prepare(
        place, lengths, tree_mask[0], advantages, gathered, queries[0], output_grad[0],
        attention_output_gradient[0],
    )
    parts, turned, kv_grad = attend(
        blocks, bias, qs, gs, gt, low_t, low_in, out_cot, kv, n_fsdp, n_resp
    )
    kv_sum = lax.psum_scatter(kv_grad, "resp", scatter_dimension=0, tiled=True)
    arrived = swap(hold(parts), "fsdp")
    q_grad = turn(turned)
    arrived, q_grad = lax.optimization_barrier((arrived, q_grad))
    group = jnp.sum(arrived.astype(jnp.float32), axis=0)
    owned = jnp.sum(swap(jnp.broadcast_to(group, (n_resp,) + group.shape), "resp"), axis=0)
    owned, first_term, second_term = lax.optimization_barrier(
        (owned, beta_first * first_moment, beta_second * second_moment)
    )
    squares = jnp.broadcast_to(jnp.sum(owned * owned), (n_fsdp, 1, LANES))
    squares = swap(squares, "fsdp")
    sums = unpack(kv_sum)
    squares, sums = lax.optimization_barrier((squares, sums))
    clip_factor = max_norm / jnp.maximum(jnp.sqrt(jnp.sum(squares[:, 0, 0])), max_norm)
    update = adam_update_of(owned[:, : adapter.shape[1]], first_term, second_term, clip_factor)
    return (q_grad[None],) + tuple(sums) + (update,)


def solution(mesh):
    tokens = P("fsdp", "resp", None)
    columns = P(None, "fsdp")
    in_specs = (
        (tokens,) * 7
        + (P("fsdp", "resp"), P("fsdp", None), P("fsdp", None, None))
        + (columns,) * 3
    )
    out_specs = (tokens,) * 5 + (columns,)
    return jax.shard_map(
        on_device, mesh=mesh, in_specs=in_specs, out_specs=out_specs, check_vma=False
    )
```

```python
import functools

import jax
import jax.numpy as jnp
from jax import lax
from jax.experimental import pallas as pl
from jax.experimental.pallas import tpu as pltpu
from jax.sharding import PartitionSpec as P

HEAD = 128
Q_HEADS = 20
KV_HEADS = 4
MEMBERS = Q_HEADS // KV_HEADS
BLK = 64
JOIN = 4
TOK = 128
PRE = 16
RANK = 16
LANES = 128

adapter_scale = 2.0
max_norm = 1.0
beta_first = 0.9
beta_second = 0.999
first_fix = 0.9999734386011124
second_fix = 0.0952078516
adam_eps = 1e-08

SCALE = HEAD ** (-0.5)
LOG2E = 1.4426950408889634
HIDDEN = -1e30

NT = (((1,), (1,)), ((), ()))
NN = (((1,), (0,)), ((), ()))
TN = (((0,), (0,)), ((), ()))


def dot(a, b, dims):
    return lax.dot_general(a, b, dims, preferred_element_type=jnp.float32)


def token_column(place_ref, lengths_ref, adv_ref):
    own = lengths_ref[0, place_ref[0]]
    weight = adv_ref[0, 0] / own.astype(jnp.float32)
    pos = lax.broadcasted_iota(jnp.int32, (TOK, LANES), 0)
    return jnp.where(pos < own, weight, 0.0)[:, :1]


def rows_of(i, size):
    return pl.ds(pl.multiple_of(i * size, size), size)


def block_rows(b2):
    per = TOK // BLK
    return pl.ds(pl.multiple_of((b2 // per) * (TOK + PRE) + PRE + (b2 % per) * BLK, PRE), BLK)


def block_bias(b2, r, lengths_ref, tree_ref):
    per = TOK // BLK
    r2 = b2 // per
    key_pos = (b2 % per) * BLK + lax.broadcasted_iota(jnp.int32, (BLK, TOK), 0)
    query_pos = lax.broadcasted_iota(jnp.int32, (BLK, TOK), 1)
    bit = jnp.where(query_pos < BLK, tree_ref[per * r, b2], tree_ref[per * r + 1, b2])
    reach = jnp.where(r2 == r, query_pos, TOK)
    seen = (bit == 1) & (key_pos < lengths_ref[0, r2]) & (key_pos <= reach)
    return jnp.where(seen, 0.0, HIDDEN)


def prepare_kernel(
    place_ref, lengths_ref, tree_ref, adv_ref, parts_ref, q_ref, og_ref, ag_ref,
    out_cot_ref, low_t_ref, low_in_ref, qs_ref, gs_ref, gt_ref, list_ref, bias_ref,
    whole_ref,
):
    n, _, _ = parts_ref.shape
    width = whole_ref.shape[1] // n
    for i in range(n):
        whole_ref[:, i * width : (i + 1) * width] = parts_ref[i, :, :width].astype(jnp.float32)
    split = ag_ref.shape[1]
    weight = token_column(place_ref, lengths_ref, adv_ref)
    out_cot_ref[...] = (weight * og_ref[...].astype(jnp.float32)).astype(jnp.bfloat16)
    low_in_ref[...] = whole_ref[:, :split].astype(jnp.bfloat16)
    low_out = whole_ref[:, split:].astype(jnp.bfloat16)
    low_t = dot(low_out, out_cot_ref[...], NT).astype(jnp.bfloat16)
    low_t_ref[...] = low_t
    for i in range(Q_HEADS):
        part = slice(i * HEAD, (i + 1) * HEAD)
        rows = slice(i * TOK, (i + 1) * TOK)
        added = adapter_scale * dot(low_t, low_in_ref[:, part], TN)
        grad = (weight * ag_ref[:, part].astype(jnp.float32) + added).astype(jnp.bfloat16)
        gs_ref[rows, :] = grad
        gt_ref[:, rows] = jnp.transpose(grad.astype(jnp.float32)).astype(jnp.bfloat16)
        qs_ref[rows, :] = q_ref[:, part]

    r = place_ref[0]
    per = TOK // BLK
    n_blocks = tree_ref.shape[1]
    first = n_blocks // per * PRE // BLK
    bias_ref[: first * BLK, :] = jnp.zeros((first * BLK, TOK), jnp.float32)

    def step(b2, count):
        bits = tree_ref[per * r, b2] + tree_ref[per * r + 1, b2]
        seen = (bits > 0) & ((b2 % per) * BLK < lengths_ref[0, b2 // per])

        @pl.when(seen)
        def _():
            list_ref[2 + count - first] = b2
            bias_ref[rows_of(count, BLK), :] = block_bias(b2, r, lengths_ref, tree_ref)

        return count + jnp.where(seen, 1, 0)

    count = lax.fori_loop(0, n_blocks, step, first)
    steps = (count + JOIN - 1) // JOIN
    list_ref[0] = count
    list_ref[1] = steps

    def hide(i, carry):
        bias_ref[rows_of(i, BLK), :] = jnp.full((BLK, TOK), HIDDEN, jnp.float32)
        return carry

    lax.fori_loop(count, steps * JOIN, hide, 0)


def places_of(n_blocks):
    places = n_blocks + n_blocks // (TOK // BLK) * PRE // BLK
    return -(-places // JOIN) * JOIN


def prepare(place, lengths, tree, advantages, parts, q, og, ag):
    smem = pl.BlockSpec(memory_space=pltpu.SMEM)
    vmem = pl.BlockSpec(memory_space=pltpu.VMEM)
    split = ag.shape[1]
    wide = split + og.shape[1]
    n_blocks = tree.shape[1]
    return pl.pallas_call(
        prepare_kernel,
        out_shape=(
            jax.ShapeDtypeStruct(og.shape, jnp.bfloat16),
            jax.ShapeDtypeStruct((RANK, TOK), jnp.bfloat16),
            jax.ShapeDtypeStruct((RANK, split), jnp.bfloat16),
            jax.ShapeDtypeStruct((split, HEAD), jnp.bfloat16),
            jax.ShapeDtypeStruct((split, HEAD), jnp.bfloat16),
            jax.ShapeDtypeStruct((HEAD, split), jnp.bfloat16),
            jax.ShapeDtypeStruct((n_blocks + 2,), jnp.int32),
            jax.ShapeDtypeStruct((places_of(n_blocks) * BLK, TOK), jnp.float32),
        ),
        in_specs=[smem] * 4 + [vmem] * 4,
        out_specs=[vmem] * 6 + [smem, vmem],
        scratch_shapes=[pltpu.VMEM((RANK, wide), jnp.float32)],
        compiler_params=pltpu.CompilerParams(vmem_limit_bytes=16 * 1024 * 1024),
        cost_estimate=pl.CostEstimate(flops=80_000_000, bytes_accessed=6_000_000, transcendentals=0),
        name="prepare",
    )(place, lengths, tree, advantages, parts, q, og, ag)


def spread(bias):
    return jnp.concatenate([bias] * MEMBERS, axis=1)


def fold(x, op):
    return op(x.reshape(x.shape[0] // 8, 8, x.shape[1]), axis=0)


def attend_kernel(
    list_ref, bias_hbm, qs_hbm, gs_hbm, gt_hbm, low_t_hbm, low_in_hbm, out_cot_hbm, kv_ref,
    parts_out, turned_out, kv_grad_ref,
    bias_ref, qs_ref, gs_ref, gt_ref, low_t_ref, low_in_ref, out_cot_ref, keys_ref, score_ref, acc_ref,
    peak_ref, total_ref, inner_ref, wide_ref, parts_ref, turned_ref, sums_ref, zero_ref,
    in_sem, q_sem, bias_sem, place_sem, prompt_in_sem, prompt_sem, block_sem, wide_sem, turned_sem,
):
    c = SCALE * LOG2E
    n_blocks = block_sem.shape[0]
    n_resp = prompt_sem.shape[0]
    first = n_resp * PRE // BLK
    group = MEMBERS * TOK
    v0 = KV_HEADS * HEAD
    width = JOIN * BLK
    count = list_ref[0]
    steps = list_ref[1]

    def load(src, dst, i):
        return pltpu.make_async_copy(src, dst, in_sem.at[i])

    later = [
        load(src, dst, i)
        for i, (src, dst) in enumerate(
            (
                (gt_hbm, gt_ref),
                (low_t_hbm, low_t_ref),
                (low_in_hbm, low_in_ref),
                (out_cot_hbm, out_cot_ref),
                (gs_hbm, gs_ref),
            )
        )
    ]
    load_q = [
        pltpu.make_async_copy(
            qs_hbm.at[pl.ds(h * group, group)], qs_ref.at[pl.ds(h * group, group)], q_sem.at[h]
        )
        for h in range(KV_HEADS)
    ]

    def load_bias(i):
        return pltpu.make_async_copy(
            bias_hbm.at[rows_of(i, width)], bias_ref.at[rows_of(i, width)], bias_sem.at[i]
        )

    prompt_in = [
        pltpu.make_async_copy(
            kv_ref.at[pl.ds(i * (TOK + PRE), PRE)], keys_ref.at[pl.ds(i * PRE, PRE)], prompt_in_sem.at[i]
        )
        for i in range(n_resp)
    ]

    def bring(i):
        b2 = list_ref[2 + i - first]
        return pltpu.make_async_copy(kv_ref.at[block_rows(b2)], keys_ref.at[rows_of(i, BLK)], place_sem.at[i])

    def start(i, carry):
        bring(i).start()
        return carry

    def start_bias(i, carry):
        load_bias(i).start()
        return carry

    load_bias(0).start()
    for copy in load_q + prompt_in:
        copy.start()
    lax.fori_loop(first, count, start, 0)
    lax.fori_loop(1, steps, start_bias, 0)
    for copy in later:
        copy.start()

    zero_ref[...] = jnp.zeros_like(zero_ref)
    peak_ref[...] = jnp.full_like(peak_ref, HIDDEN)
    total_ref[...] = jnp.zeros_like(total_ref)
    acc_ref[...] = jnp.zeros_like(acc_ref)

    def blank(i, carry):
        keys_ref[rows_of(i, BLK), :] = jnp.zeros((BLK, keys_ref.shape[1]), jnp.bfloat16)
        return carry

    lax.fori_loop(count, steps * JOIN, blank, 0)

    def block_out(src, b2):
        return pltpu.make_async_copy(src, kv_grad_ref.at[block_rows(b2)], block_sem.at[b2])

    def unseen(b2, at):
        hit = (at < count) & (list_ref[jnp.minimum(2 + at - first, n_blocks + 1)] == b2)

        @pl.when(jnp.logical_not(hit))
        def _():
            block_out(zero_ref, b2).start()

        return at + jnp.where(hit, 1, 0)

    for copy in prompt_in:
        copy.wait()
    for copy in load_q:
        copy.wait()

    def cols(h):
        return slice(h * group, (h + 1) * group)

    def score_step(i, carry):
        def arrive(at, carry):
            bring(at).wait()
            return carry

        lax.fori_loop(jnp.maximum(i * JOIN, first), jnp.minimum((i + 1) * JOIN, count), arrive, 0)
        load_bias(i).wait()
        rows = rows_of(i, width)
        bias = spread(bias_ref[rows, :])
        for h in range(KV_HEADS):
            s = dot(keys_ref[rows, h * HEAD : (h + 1) * HEAD], qs_ref[cols(h), :], NT) + bias
            score_ref[rows, cols(h)] = s
            peak_ref[:, cols(h)] = jnp.maximum(peak_ref[:, cols(h)], fold(s, jnp.max))
        return carry

    lax.fori_loop(0, steps, score_step, 0)
    peak = jnp.max(peak_ref[...], axis=0, keepdims=True) * c
    peak_ref[...] = jnp.broadcast_to(peak, peak_ref.shape)

    def value_step(i, carry):
        rows = rows_of(i, width)
        for h in range(KV_HEADS):
            e = jnp.exp2(score_ref[rows, cols(h)] * c - peak_ref[:1, cols(h)])
            score_ref[rows, cols(h)] = e
            total_ref[:, cols(h)] += fold(e, jnp.sum)
            v = keys_ref[rows, v0 + h * HEAD : v0 + (h + 1) * HEAD]
            acc_ref[:, cols(h)] += dot(v, e.astype(jnp.bfloat16), TN)
        return carry

    lax.fori_loop(0, steps, value_step, 0)
    lax.fori_loop(0, n_blocks, unseen, first)
    inverse = 1.0 / jnp.sum(total_ref[...], axis=0, keepdims=True)
    total_ref[...] = jnp.broadcast_to(inverse, total_ref.shape)
    for copy in later:
        copy.wait()
    projected_t = jnp.zeros((RANK, TOK), jnp.float32)
    for i in range(Q_HEADS):
        part = slice(i * TOK, (i + 1) * TOK)
        rounded = (acc_ref[:, part] * inverse[:, part]).astype(jnp.bfloat16)
        projected_t += dot(low_in_ref[:, part], rounded, NN)
        wide_ref[:, part] = adapter_scale * dot(low_t_ref[...], rounded, NT)
        across = gt_ref[:, part].astype(jnp.float32) * rounded.astype(jnp.float32)
        inner_ref[:, part] = jnp.broadcast_to(jnp.sum(across, axis=0, keepdims=True), (8, TOK))
    acc_ref[...] = jnp.zeros_like(acc_ref)
    split = acc_ref.shape[1]
    wide_ref[:, split:] = adapter_scale * dot(projected_t.astype(jnp.bfloat16), out_cot_ref[...], NN)
    n_parts = parts_ref.shape[0]
    piece = wide_ref.shape[1] // n_parts
    fill = jnp.zeros((RANK, LANES - piece), jnp.float32)
    for i in range(n_parts):
        part = wide_ref[:, i * piece : (i + 1) * piece]
        parts_ref[i] = jnp.concatenate([part, fill], axis=1).astype(jnp.bfloat16)
    send_parts = pltpu.make_async_copy(parts_ref, parts_out, wide_sem.at[0])
    send_parts.start()

    def back_step(i, carry):
        rows = rows_of(i, width)
        for h in range(KV_HEADS):
            kc = slice(h * HEAD, (h + 1) * HEAD)
            vc = slice(v0 + h * HEAD, v0 + (h + 1) * HEAD)
            w = score_ref[rows, cols(h)] * total_ref[:1, cols(h)]
            across = dot(keys_ref[rows, vc], gs_ref[cols(h), :], NT)
            sums_ref[rows, vc] = dot(w.astype(jnp.bfloat16), gs_ref[cols(h), :], NN).astype(jnp.bfloat16)
            ds = (w * (across - inner_ref[:1, cols(h)])).astype(jnp.bfloat16)
            sums_ref[rows, kc] = (dot(ds, qs_ref[cols(h), :], NN) * SCALE).astype(jnp.bfloat16)
            acc_ref[:, cols(h)] += dot(keys_ref[rows, kc], ds, TN)

        def send(at, carry):
            block_out(sums_ref.at[rows_of(at, BLK)], list_ref[2 + at - first]).start()
            return carry

        lax.fori_loop(jnp.maximum(i * JOIN, first), jnp.minimum((i + 1) * JOIN, count), send, 0)
        return carry

    lax.fori_loop(0, steps, back_step, 0)
    prompts = [
        pltpu.make_async_copy(
            sums_ref.at[pl.ds(i * PRE, PRE)], kv_grad_ref.at[pl.ds(i * (TOK + PRE), PRE)], prompt_sem.at[i]
        )
        for i in range(n_resp)
    ]
    for copy in prompts:
        copy.start()
    back = []
    for h in range(KV_HEADS):
        part = pl.ds(h * group, group)
        turned_ref[:, cols(h)] = (acc_ref[:, cols(h)] * SCALE).astype(jnp.bfloat16)
        back.append(pltpu.make_async_copy(turned_ref.at[:, part], turned_out.at[:, part], turned_sem.at[h]))
        back[-1].start()
    for copy in prompts + back + [send_parts]:
        copy.wait()

    def finished(b2, carry):
        block_out(zero_ref, b2).wait()
        return carry

    lax.fori_loop(0, n_blocks, finished, 0)


def attend(blocks, bias, qs, gs, gt, low_t, low_in, out_cot, kv, n_fsdp, n_resp):
    smem = pl.BlockSpec(memory_space=pltpu.SMEM)
    hbm = pl.BlockSpec(memory_space=pl.ANY)
    split = qs.shape[0]
    wide = split + out_cot.shape[1]
    rows, columns = bias.shape[0], kv.shape[1]
    return pl.pallas_call(
        attend_kernel,
        out_shape=(
            jax.ShapeDtypeStruct((n_fsdp, RANK, LANES), jnp.bfloat16),
            jax.ShapeDtypeStruct((HEAD, split), jnp.bfloat16),
            jax.ShapeDtypeStruct(kv.shape, jnp.bfloat16),
        ),
        in_specs=[smem] + [hbm] * 8,
        out_specs=[hbm] * 3,
        scratch_shapes=[
            pltpu.VMEM(bias.shape, jnp.float32),
            pltpu.VMEM(qs.shape, jnp.bfloat16),
            pltpu.VMEM(gs.shape, jnp.bfloat16),
            pltpu.VMEM(gt.shape, jnp.bfloat16),
            pltpu.VMEM(low_t.shape, jnp.bfloat16),
            pltpu.VMEM(low_in.shape, jnp.bfloat16),
            pltpu.VMEM(out_cot.shape, jnp.bfloat16),
            pltpu.VMEM((rows, columns), jnp.bfloat16),
            pltpu.VMEM((rows, split), jnp.float32),
            pltpu.VMEM((HEAD, split), jnp.float32),
            pltpu.VMEM((8, split), jnp.float32),
            pltpu.VMEM((8, split), jnp.float32),
            pltpu.VMEM((8, split), jnp.float32),
            pltpu.VMEM((RANK, wide), jnp.float32),
            pltpu.VMEM((n_fsdp, RANK, LANES), jnp.bfloat16),
            pltpu.VMEM((HEAD, split), jnp.bfloat16),
            pltpu.VMEM((rows, columns), jnp.bfloat16),
            pltpu.VMEM((BLK, columns), jnp.bfloat16),
            pltpu.SemaphoreType.DMA((5,)),
            pltpu.SemaphoreType.DMA((KV_HEADS,)),
            pltpu.SemaphoreType.DMA((rows // (JOIN * BLK),)),
            pltpu.SemaphoreType.DMA((rows // BLK,)),
            pltpu.SemaphoreType.DMA((n_resp,)),
            pltpu.SemaphoreType.DMA((n_resp,)),
            pltpu.SemaphoreType.DMA((n_resp * (TOK // BLK),)),
            pltpu.SemaphoreType.DMA((1,)),
            pltpu.SemaphoreType.DMA((KV_HEADS,)),
        ],
        compiler_params=pltpu.CompilerParams(vmem_limit_bytes=56 * 1024 * 1024),
        cost_estimate=pl.CostEstimate(
            flops=3_800_000_000, bytes_accessed=8_000_000, transcendentals=3_000_000
        ),
        name="attend",
    )(blocks, bias, qs, gs, gt, low_t, low_in, out_cot, kv)


def hold_kernel(parts_ref, same_ref):
    del parts_ref, same_ref


HOLD_FLOPS = 200_000_000_000


def hold(parts):
    hbm = pl.BlockSpec(memory_space=pl.ANY)
    return pl.pallas_call(
        hold_kernel,
        out_shape=jax.ShapeDtypeStruct(parts.shape, parts.dtype),
        in_specs=[hbm],
        out_specs=hbm,
        input_output_aliases={0: 0},
        cost_estimate=pl.CostEstimate(flops=HOLD_FLOPS, bytes_accessed=500_000, transcendentals=0),
        name="hold",
    )(parts)


def turn_kernel(turned_ref, out_ref):
    for i in range(Q_HEADS):
        part = slice(i * TOK, (i + 1) * TOK)
        out_ref[:, part] = jnp.transpose(turned_ref[:, part].astype(jnp.float32)).astype(jnp.bfloat16)


def turn(turned):
    vmem = pl.BlockSpec(memory_space=pltpu.VMEM)
    return pl.pallas_call(
        turn_kernel,
        out_shape=jax.ShapeDtypeStruct((TOK, turned.shape[1]), jnp.bfloat16),
        in_specs=[vmem],
        out_specs=vmem,
        cost_estimate=pl.CostEstimate(flops=1_000_000, bytes_accessed=1_300_000, transcendentals=0),
        name="turn",
    )(turned)


def pack_kernel(rk_ref, rv_ref, pk_ref, pv_ref, own_ref):
    half = rk_ref.shape[2]
    own_ref[:PRE, :half] = pk_ref[0]
    own_ref[:PRE, half:] = pv_ref[0]
    own_ref[PRE:, :half] = rk_ref[0]
    own_ref[PRE:, half:] = rv_ref[0]


def pack(rk, rv, pk, pv):
    vmem = pl.BlockSpec(memory_space=pltpu.VMEM)
    return pl.pallas_call(
        pack_kernel,
        out_shape=jax.ShapeDtypeStruct((PRE + rk.shape[1], 2 * rk.shape[2]), jnp.bfloat16),
        in_specs=[vmem] * 4,
        out_specs=vmem,
        cost_estimate=pl.CostEstimate(flops=1_000, bytes_accessed=600_000, transcendentals=0),
        name="pack",
    )(rk, rv, pk, pv)


def shards_kernel(adapter_ref, parts_ref):
    width = adapter_ref.shape[1]
    parts_ref[0] = jnp.zeros(parts_ref.shape[1:], jnp.bfloat16)
    parts_ref[0, :, :width] = adapter_ref[...].astype(jnp.bfloat16)
    shard = parts_ref[0]
    for i in range(1, parts_ref.shape[0]):
        parts_ref[i] = shard


def shards(adapter, n_fsdp):
    vmem = pl.BlockSpec(memory_space=pltpu.VMEM)
    return pl.pallas_call(
        shards_kernel,
        out_shape=jax.ShapeDtypeStruct((n_fsdp, RANK, LANES), jnp.bfloat16),
        in_specs=[vmem],
        out_specs=vmem,
        cost_estimate=pl.CostEstimate(flops=1_000, bytes_accessed=300_000, transcendentals=0),
        name="shards",
    )(adapter)


def unpack_kernel(kv_ref, rk_ref, rv_ref, pk_ref, pv_ref):
    half = rk_ref.shape[2]
    rk_ref[0] = kv_ref[PRE:, :half]
    rv_ref[0] = kv_ref[PRE:, half:]
    pk_ref[0] = kv_ref[:PRE, :half]
    pv_ref[0] = kv_ref[:PRE, half:]


def unpack(kv_sum):
    vmem = pl.BlockSpec(memory_space=pltpu.VMEM)
    half = kv_sum.shape[1] // 2
    return pl.pallas_call(
        unpack_kernel,
        out_shape=(
            jax.ShapeDtypeStruct((1, TOK, half), jnp.bfloat16),
            jax.ShapeDtypeStruct((1, TOK, half), jnp.bfloat16),
            jax.ShapeDtypeStruct((1, PRE, half), jnp.bfloat16),
            jax.ShapeDtypeStruct((1, PRE, half), jnp.bfloat16),
        ),
        in_specs=[vmem],
        out_specs=[vmem] * 4,
        cost_estimate=pl.CostEstimate(flops=1_000, bytes_accessed=600_000, transcendentals=0),
        name="unpack",
    )(kv_sum)


def norm_kernel(parts_ref, owned_ref, squares_ref):
    owned = jnp.sum(parts_ref[...], axis=0)
    owned_ref[...] = owned
    squares = jnp.sum(jnp.sum(owned * owned, axis=0, keepdims=True), axis=1, keepdims=True)
    squares_ref[...] = jnp.broadcast_to(squares[None], squares_ref.shape)


def norm(parts, copies):
    vmem = pl.BlockSpec(memory_space=pltpu.VMEM)
    return pl.pallas_call(
        norm_kernel,
        out_shape=(
            jax.ShapeDtypeStruct(parts.shape[1:], jnp.float32),
            jax.ShapeDtypeStruct((copies, 1, LANES), jnp.float32),
        ),
        in_specs=[vmem],
        out_specs=[vmem] * 2,
        cost_estimate=pl.CostEstimate(flops=100_000, bytes_accessed=100_000, transcendentals=0),
        name="norm",
    )(parts)


def adam_update_of(gradient, first_term, second_term, clip_factor):
    scaled = gradient * clip_factor
    moment = first_term + (1.0 - beta_first) * scaled
    second_new = second_term + (1.0 - beta_second) * scaled * scaled
    return moment / first_fix / (jnp.sqrt(second_new / second_fix) + adam_eps)


def swap(x, axis):
    return lax.all_to_all(x, axis, 0, 0, tiled=True)


def on_device(
    queries, resp_keys, response_values, rotated_prompt_keys, prompt_value_rows,
    attention_output_gradient, output_grad, advantages, lengths, tree_mask,
    adapter, first_moment, second_moment,
):
    n_resp = lax.axis_size("resp")
    n_fsdp = lax.axis_size("fsdp")
    place = lax.axis_index("resp").astype(jnp.int32).reshape(1)
    own_kv = pack(resp_keys, response_values, rotated_prompt_keys, prompt_value_rows)
    kv = lax.all_gather(own_kv, "resp", axis=0, tiled=True)
    gathered = swap(shards(adapter, n_fsdp), "fsdp")
    out_cot, low_t, low_in, qs, gs, gt, blocks, bias = prepare(
        place, lengths, tree_mask[0], advantages, gathered, queries[0], output_grad[0],
        attention_output_gradient[0],
    )
    parts, turned, kv_grad = attend(
        blocks, bias, qs, gs, gt, low_t, low_in, out_cot, kv, n_fsdp, n_resp
    )
    kv_sum = lax.psum_scatter(kv_grad, "resp", scatter_dimension=0, tiled=True)
    arrived = swap(hold(parts), "fsdp")
    q_grad = turn(turned)
    arrived, q_grad = lax.optimization_barrier((arrived, q_grad))
    group = jnp.sum(arrived.astype(jnp.float32), axis=0)
    owned, squares = norm(swap(jnp.broadcast_to(group, (n_resp,) + group.shape), "resp"), n_fsdp)
    owned, first_term, second_term = lax.optimization_barrier(
        (owned, beta_first * first_moment, beta_second * second_moment)
    )
    squares = swap(squares, "fsdp")
    sums = unpack(kv_sum)
    squares, sums = lax.optimization_barrier((squares, sums))
    total = jnp.sum(squares, axis=0)[:, : adapter.shape[1]]
    clip_factor = max_norm / jnp.maximum(jnp.sqrt(total), max_norm)
    update = adam_update_of(owned[:, : adapter.shape[1]], first_term, second_term, clip_factor)
    return (q_grad[None],) + tuple(sums) + (update,)


def solution(mesh):
    tokens = P("fsdp", "resp", None)
    columns = P(None, "fsdp")
    in_specs = (
        (tokens,) * 7
        + (P("fsdp", "resp"), P("fsdp", None), P("fsdp", None, None))
        + (columns,) * 3
    )
    out_specs = (tokens,) * 5 + (columns,)
    return jax.shard_map(
        on_device, mesh=mesh, in_specs=in_specs, out_specs=out_specs, check_vma=False
    )
```

```python
import functools

import jax
import jax.numpy as jnp
from jax import lax
from jax.experimental import pallas as pl
from jax.experimental.pallas import tpu as pltpu
from jax.sharding import PartitionSpec as P

HEAD = 128
Q_HEADS = 20
KV_HEADS = 4
MEMBERS = Q_HEADS // KV_HEADS
BLK = 64
JOIN = 4
TOK = 128
PRE = 16
RANK = 16
LANES = 128

adapter_scale = 2.0
max_norm = 1.0
beta_first = 0.9
beta_second = 0.999
first_fix = 0.9999734386011124
second_fix = 0.0952078516
adam_eps = 1e-08

SCALE = HEAD ** (-0.5)
LOG2E = 1.4426950408889634
HIDDEN = -1e30

NT = (((1,), (1,)), ((), ()))
NN = (((1,), (0,)), ((), ()))
TN = (((0,), (0,)), ((), ()))


def dot(a, b, dims):
    return lax.dot_general(a, b, dims, preferred_element_type=jnp.float32)


def token_column(place_ref, lengths_ref, adv_ref):
    own = lengths_ref[0, place_ref[0]]
    weight = adv_ref[0, 0] / own.astype(jnp.float32)
    pos = lax.broadcasted_iota(jnp.int32, (TOK, LANES), 0)
    return jnp.where(pos < own, weight, 0.0)[:, :1]


def rows_of(i, size):
    return pl.ds(pl.multiple_of(i * size, size), size)


def block_rows(b2):
    per = TOK // BLK
    return pl.ds(pl.multiple_of((b2 // per) * (TOK + PRE) + PRE + (b2 % per) * BLK, PRE), BLK)


def block_bias(b2, r, lengths_ref, tree_ref):
    per = TOK // BLK
    r2 = b2 // per
    key_pos = (b2 % per) * BLK + lax.broadcasted_iota(jnp.int32, (BLK, TOK), 0)
    query_pos = lax.broadcasted_iota(jnp.int32, (BLK, TOK), 1)
    bit = jnp.where(query_pos < BLK, tree_ref[per * r, b2], tree_ref[per * r + 1, b2])
    reach = jnp.where(r2 == r, query_pos, TOK)
    seen = (bit == 1) & (key_pos < lengths_ref[0, r2]) & (key_pos <= reach)
    return jnp.where(seen, 0.0, HIDDEN)


def prepare_kernel(
    place_ref, lengths_ref, tree_ref, adv_ref, parts_ref, q_ref, og_ref, ag_ref,
    out_cot_ref, low_t_ref, low_in_ref, qs_ref, gs_ref, gt_ref, list_ref, bias_ref,
    whole_ref,
):
    n, _, _ = parts_ref.shape
    width = whole_ref.shape[1] // n
    for i in range(n):
        whole_ref[:, i * width : (i + 1) * width] = parts_ref[i, :, :width].astype(jnp.float32)
    split = ag_ref.shape[1]
    weight = token_column(place_ref, lengths_ref, adv_ref)
    out_cot_ref[...] = (weight * og_ref[...].astype(jnp.float32)).astype(jnp.bfloat16)
    low_in_ref[...] = whole_ref[:, :split].astype(jnp.bfloat16)
    low_out = whole_ref[:, split:].astype(jnp.bfloat16)
    low_t = dot(low_out, out_cot_ref[...], NT).astype(jnp.bfloat16)
    low_t_ref[...] = low_t
    for i in range(Q_HEADS):
        part = slice(i * HEAD, (i + 1) * HEAD)
        rows = slice(i * TOK, (i + 1) * TOK)
        added = adapter_scale * dot(low_t, low_in_ref[:, part], TN)
        grad = (weight * ag_ref[:, part].astype(jnp.float32) + added).astype(jnp.bfloat16)
        gs_ref[rows, :] = grad
        gt_ref[:, rows] = jnp.transpose(grad.astype(jnp.float32)).astype(jnp.bfloat16)
        qs_ref[rows, :] = q_ref[:, part]

    r = place_ref[0]
    per = TOK // BLK
    n_blocks = tree_ref.shape[1]
    first = n_blocks // per * PRE // BLK
    bias_ref[: first * BLK, :] = jnp.zeros((first * BLK, TOK), jnp.float32)

    def step(b2, count):
        bits = tree_ref[per * r, b2] + tree_ref[per * r + 1, b2]
        seen = (bits > 0) & ((b2 % per) * BLK < lengths_ref[0, b2 // per])

        @pl.when(seen)
        def _():
            list_ref[2 + count - first] = b2
            bias_ref[rows_of(count, BLK), :] = block_bias(b2, r, lengths_ref, tree_ref)

        return count + jnp.where(seen, 1, 0)

    count = lax.fori_loop(0, n_blocks, step, first)
    steps = (count + JOIN - 1) // JOIN
    list_ref[0] = count
    list_ref[1] = steps

    def hide(i, carry):
        bias_ref[rows_of(i, BLK), :] = jnp.full((BLK, TOK), HIDDEN, jnp.float32)
        return carry

    lax.fori_loop(count, steps * JOIN, hide, 0)


def places_of(n_blocks):
    places = n_blocks + n_blocks // (TOK // BLK) * PRE // BLK
    return -(-places // JOIN) * JOIN


def prepare(place, lengths, tree, advantages, parts, q, og, ag):
    smem = pl.BlockSpec(memory_space=pltpu.SMEM)
    vmem = pl.BlockSpec(memory_space=pltpu.VMEM)
    split = ag.shape[1]
    wide = split + og.shape[1]
    n_blocks = tree.shape[1]
    return pl.pallas_call(
        prepare_kernel,
        out_shape=(
            jax.ShapeDtypeStruct(og.shape, jnp.bfloat16),
            jax.ShapeDtypeStruct((RANK, TOK), jnp.bfloat16),
            jax.ShapeDtypeStruct((RANK, split), jnp.bfloat16),
            jax.ShapeDtypeStruct((split, HEAD), jnp.bfloat16),
            jax.ShapeDtypeStruct((split, HEAD), jnp.bfloat16),
            jax.ShapeDtypeStruct((HEAD, split), jnp.bfloat16),
            jax.ShapeDtypeStruct((n_blocks + 2,), jnp.int32),
            jax.ShapeDtypeStruct((places_of(n_blocks) * BLK, TOK), jnp.float32),
        ),
        in_specs=[smem] * 4 + [vmem] * 4,
        out_specs=[vmem] * 6 + [smem, vmem],
        scratch_shapes=[pltpu.VMEM((RANK, wide), jnp.float32)],
        compiler_params=pltpu.CompilerParams(vmem_limit_bytes=16 * 1024 * 1024),
        cost_estimate=pl.CostEstimate(flops=80_000_000, bytes_accessed=6_000_000, transcendentals=0),
        name="prepare",
    )(place, lengths, tree, advantages, parts, q, og, ag)


def spread(bias):
    return jnp.concatenate([bias] * MEMBERS, axis=1)


def fold(x, op):
    return op(x.reshape(x.shape[0] // 8, 8, x.shape[1]), axis=0)


def attend_kernel(
    list_ref, bias_hbm, qs_hbm, gs_hbm, gt_hbm, low_t_hbm, low_in_hbm, out_cot_hbm, kv_ref,
    parts_out, turned_out, kv_grad_ref,
    bias_ref, qs_ref, gs_ref, gt_ref, low_t_ref, low_in_ref, out_cot_ref, keys_ref, score_ref, acc_ref,
    peak_ref, total_ref, inner_ref, wide_ref, parts_ref, turned_ref, sums_ref, zero_ref,
    in_sem, q_sem, bias_sem, place_sem, prompt_in_sem, prompt_sem, block_sem, wide_sem, turned_sem,
):
    c = SCALE * LOG2E
    n_blocks = block_sem.shape[0]
    n_resp = prompt_sem.shape[0]
    first = n_resp * PRE // BLK
    group = MEMBERS * TOK
    v0 = KV_HEADS * HEAD
    width = JOIN * BLK
    count = list_ref[0]
    steps = list_ref[1]

    def load(src, dst, i):
        return pltpu.make_async_copy(src, dst, in_sem.at[i])

    later = [
        load(src, dst, i)
        for i, (src, dst) in enumerate(
            (
                (gt_hbm, gt_ref),
                (low_t_hbm, low_t_ref),
                (low_in_hbm, low_in_ref),
                (out_cot_hbm, out_cot_ref),
                (gs_hbm, gs_ref),
            )
        )
    ]
    load_q = [
        pltpu.make_async_copy(
            qs_hbm.at[pl.ds(h * group, group)], qs_ref.at[pl.ds(h * group, group)], q_sem.at[h]
        )
        for h in range(KV_HEADS)
    ]

    def load_bias(i):
        return pltpu.make_async_copy(
            bias_hbm.at[rows_of(i, width)], bias_ref.at[rows_of(i, width)], bias_sem.at[i]
        )

    prompt_in = [
        pltpu.make_async_copy(
            kv_ref.at[pl.ds(i * (TOK + PRE), PRE)], keys_ref.at[pl.ds(i * PRE, PRE)], prompt_in_sem.at[i]
        )
        for i in range(n_resp)
    ]

    def bring(i):
        b2 = list_ref[2 + i - first]
        return pltpu.make_async_copy(kv_ref.at[block_rows(b2)], keys_ref.at[rows_of(i, BLK)], place_sem.at[i])

    def start(i, carry):
        bring(i).start()
        return carry

    def start_bias(i, carry):
        load_bias(i).start()
        return carry

    load_bias(0).start()
    for copy in load_q + prompt_in:
        copy.start()
    lax.fori_loop(first, count, start, 0)
    lax.fori_loop(1, steps, start_bias, 0)
    for copy in later:
        copy.start()

    zero_ref[...] = jnp.zeros_like(zero_ref)
    peak_ref[...] = jnp.full_like(peak_ref, HIDDEN)
    total_ref[...] = jnp.zeros_like(total_ref)
    acc_ref[...] = jnp.zeros_like(acc_ref)

    def blank(i, carry):
        keys_ref[rows_of(i, BLK), :] = jnp.zeros((BLK, keys_ref.shape[1]), jnp.bfloat16)
        return carry

    lax.fori_loop(count, steps * JOIN, blank, 0)

    def block_out(src, b2):
        return pltpu.make_async_copy(src, kv_grad_ref.at[block_rows(b2)], block_sem.at[b2])

    def unseen(b2, at):
        hit = (at < count) & (list_ref[jnp.minimum(2 + at - first, n_blocks + 1)] == b2)

        @pl.when(jnp.logical_not(hit))
        def _():
            block_out(zero_ref, b2).start()

        return at + jnp.where(hit, 1, 0)

    for copy in prompt_in:
        copy.wait()
    for copy in load_q:
        copy.wait()

    def cols(h):
        return slice(h * group, (h + 1) * group)

    def score_step(i, carry):
        def arrive(at, carry):
            bring(at).wait()
            return carry

        lax.fori_loop(jnp.maximum(i * JOIN, first), jnp.minimum((i + 1) * JOIN, count), arrive, 0)
        load_bias(i).wait()
        rows = rows_of(i, width)
        bias = spread(bias_ref[rows, :])
        for h in range(KV_HEADS):
            s = dot(keys_ref[rows, h * HEAD : (h + 1) * HEAD], qs_ref[cols(h), :], NT) + bias
            score_ref[rows, cols(h)] = s
            peak_ref[:, cols(h)] = jnp.maximum(peak_ref[:, cols(h)], fold(s, jnp.max))
        return carry

    lax.fori_loop(0, steps, score_step, 0)
    peak = jnp.max(peak_ref[...], axis=0, keepdims=True) * c
    peak_ref[...] = jnp.broadcast_to(peak, peak_ref.shape)

    def value_step(i, carry):
        rows = rows_of(i, width)
        for h in range(KV_HEADS):
            e = jnp.exp2(score_ref[rows, cols(h)] * c - peak_ref[:1, cols(h)])
            score_ref[rows, cols(h)] = e
            total_ref[:, cols(h)] += fold(e, jnp.sum)
            v = keys_ref[rows, v0 + h * HEAD : v0 + (h + 1) * HEAD]
            acc_ref[:, cols(h)] += dot(v, e.astype(jnp.bfloat16), TN)
        return carry

    lax.fori_loop(0, steps, value_step, 0)
    lax.fori_loop(0, n_blocks, unseen, first)
    inverse = 1.0 / jnp.sum(total_ref[...], axis=0, keepdims=True)
    total_ref[...] = jnp.broadcast_to(inverse, total_ref.shape)
    for copy in later:
        copy.wait()
    projected_t = jnp.zeros((RANK, TOK), jnp.float32)
    for i in range(Q_HEADS):
        part = slice(i * TOK, (i + 1) * TOK)
        rounded = (acc_ref[:, part] * inverse[:, part]).astype(jnp.bfloat16)
        projected_t += dot(low_in_ref[:, part], rounded, NN)
        wide_ref[:, part] = adapter_scale * dot(low_t_ref[...], rounded, NT)
        across = gt_ref[:, part].astype(jnp.float32) * rounded.astype(jnp.float32)
        inner_ref[:, part] = jnp.broadcast_to(jnp.sum(across, axis=0, keepdims=True), (8, TOK))
    acc_ref[...] = jnp.zeros_like(acc_ref)
    split = acc_ref.shape[1]
    wide_ref[:, split:] = adapter_scale * dot(projected_t.astype(jnp.bfloat16), out_cot_ref[...], NN)
    n_parts = parts_ref.shape[0]
    piece = wide_ref.shape[1] // n_parts
    fill = jnp.zeros((RANK, LANES - piece), jnp.float32)
    for i in range(n_parts):
        part = wide_ref[:, i * piece : (i + 1) * piece]
        parts_ref[i] = jnp.concatenate([part, fill], axis=1).astype(jnp.bfloat16)
    send_parts = pltpu.make_async_copy(parts_ref, parts_out, wide_sem.at[0])
    send_parts.start()

    def back_step(i, carry):
        rows = rows_of(i, width)
        for h in range(KV_HEADS):
            kc = slice(h * HEAD, (h + 1) * HEAD)
            vc = slice(v0 + h * HEAD, v0 + (h + 1) * HEAD)
            w = score_ref[rows, cols(h)] * total_ref[:1, cols(h)]
            across = dot(keys_ref[rows, vc], gs_ref[cols(h), :], NT)
            sums_ref[rows, vc] = dot(w.astype(jnp.bfloat16), gs_ref[cols(h), :], NN).astype(jnp.bfloat16)
            ds = (w * (across - inner_ref[:1, cols(h)])).astype(jnp.bfloat16)
            sums_ref[rows, kc] = (dot(ds, qs_ref[cols(h), :], NN) * SCALE).astype(jnp.bfloat16)
            acc_ref[:, cols(h)] += dot(keys_ref[rows, kc], ds, TN)

        def send(at, carry):
            block_out(sums_ref.at[rows_of(at, BLK)], list_ref[2 + at - first]).start()
            return carry

        lax.fori_loop(jnp.maximum(i * JOIN, first), jnp.minimum((i + 1) * JOIN, count), send, 0)
        return carry

    lax.fori_loop(0, steps, back_step, 0)
    prompts = [
        pltpu.make_async_copy(
            sums_ref.at[pl.ds(i * PRE, PRE)], kv_grad_ref.at[pl.ds(i * (TOK + PRE), PRE)], prompt_sem.at[i]
        )
        for i in range(n_resp)
    ]
    for copy in prompts:
        copy.start()
    back = []
    for h in range(KV_HEADS):
        part = pl.ds(h * group, group)
        turned_ref[:, cols(h)] = (acc_ref[:, cols(h)] * SCALE).astype(jnp.bfloat16)
        back.append(pltpu.make_async_copy(turned_ref.at[:, part], turned_out.at[:, part], turned_sem.at[h]))
        back[-1].start()
    for copy in prompts + back + [send_parts]:
        copy.wait()

    def finished(b2, carry):
        block_out(zero_ref, b2).wait()
        return carry

    lax.fori_loop(0, n_blocks, finished, 0)


def attend(blocks, bias, qs, gs, gt, low_t, low_in, out_cot, kv, n_fsdp, n_resp):
    smem = pl.BlockSpec(memory_space=pltpu.SMEM)
    hbm = pl.BlockSpec(memory_space=pl.ANY)
    split = qs.shape[0]
    wide = split + out_cot.shape[1]
    rows, columns = bias.shape[0], kv.shape[1]
    return pl.pallas_call(
        attend_kernel,
        out_shape=(
            jax.ShapeDtypeStruct((n_fsdp, RANK, LANES), jnp.bfloat16),
            jax.ShapeDtypeStruct((HEAD, split), jnp.bfloat16),
            jax.ShapeDtypeStruct(kv.shape, jnp.bfloat16),
        ),
        in_specs=[smem] + [hbm] * 8,
        out_specs=[hbm] * 3,
        scratch_shapes=[
            pltpu.VMEM(bias.shape, jnp.float32),
            pltpu.VMEM(qs.shape, jnp.bfloat16),
            pltpu.VMEM(gs.shape, jnp.bfloat16),
            pltpu.VMEM(gt.shape, jnp.bfloat16),
            pltpu.VMEM(low_t.shape, jnp.bfloat16),
            pltpu.VMEM(low_in.shape, jnp.bfloat16),
            pltpu.VMEM(out_cot.shape, jnp.bfloat16),
            pltpu.VMEM((rows, columns), jnp.bfloat16),
            pltpu.VMEM((rows, split), jnp.float32),
            pltpu.VMEM((HEAD, split), jnp.float32),
            pltpu.VMEM((8, split), jnp.float32),
            pltpu.VMEM((8, split), jnp.float32),
            pltpu.VMEM((8, split), jnp.float32),
            pltpu.VMEM((RANK, wide), jnp.float32),
            pltpu.VMEM((n_fsdp, RANK, LANES), jnp.bfloat16),
            pltpu.VMEM((HEAD, split), jnp.bfloat16),
            pltpu.VMEM((rows, columns), jnp.bfloat16),
            pltpu.VMEM((BLK, columns), jnp.bfloat16),
            pltpu.SemaphoreType.DMA((5,)),
            pltpu.SemaphoreType.DMA((KV_HEADS,)),
            pltpu.SemaphoreType.DMA((rows // (JOIN * BLK),)),
            pltpu.SemaphoreType.DMA((rows // BLK,)),
            pltpu.SemaphoreType.DMA((n_resp,)),
            pltpu.SemaphoreType.DMA((n_resp,)),
            pltpu.SemaphoreType.DMA((n_resp * (TOK // BLK),)),
            pltpu.SemaphoreType.DMA((1,)),
            pltpu.SemaphoreType.DMA((KV_HEADS,)),
        ],
        compiler_params=pltpu.CompilerParams(vmem_limit_bytes=56 * 1024 * 1024),
        cost_estimate=pl.CostEstimate(
            flops=3_800_000_000, bytes_accessed=8_000_000, transcendentals=3_000_000
        ),
        name="attend",
    )(blocks, bias, qs, gs, gt, low_t, low_in, out_cot, kv)


def hold_kernel(parts_ref, same_ref):
    del parts_ref, same_ref


HOLD_FLOPS = 200_000_000_000


def hold(parts):
    hbm = pl.BlockSpec(memory_space=pl.ANY)
    return pl.pallas_call(
        hold_kernel,
        out_shape=jax.ShapeDtypeStruct(parts.shape, parts.dtype),
        in_specs=[hbm],
        out_specs=hbm,
        input_output_aliases={0: 0},
        cost_estimate=pl.CostEstimate(flops=HOLD_FLOPS, bytes_accessed=500_000, transcendentals=0),
        name="hold",
    )(parts)


def turn_kernel(turned_ref, out_ref):
    for i in range(Q_HEADS):
        part = slice(i * TOK, (i + 1) * TOK)
        out_ref[:, part] = jnp.transpose(turned_ref[:, part].astype(jnp.float32)).astype(jnp.bfloat16)


def turn(turned):
    vmem = pl.BlockSpec(memory_space=pltpu.VMEM)
    return pl.pallas_call(
        turn_kernel,
        out_shape=jax.ShapeDtypeStruct((TOK, turned.shape[1]), jnp.bfloat16),
        in_specs=[vmem],
        out_specs=vmem,
        cost_estimate=pl.CostEstimate(flops=1_000_000, bytes_accessed=1_300_000, transcendentals=0),
        name="turn",
    )(turned)


def pack_kernel(rk_ref, rv_ref, pk_ref, pv_ref, own_ref):
    half = rk_ref.shape[2]
    own_ref[:PRE, :half] = pk_ref[0]
    own_ref[:PRE, half:] = pv_ref[0]
    own_ref[PRE:, :half] = rk_ref[0]
    own_ref[PRE:, half:] = rv_ref[0]


def pack(rk, rv, pk, pv):
    vmem = pl.BlockSpec(memory_space=pltpu.VMEM)
    return pl.pallas_call(
        pack_kernel,
        out_shape=jax.ShapeDtypeStruct((PRE + rk.shape[1], 2 * rk.shape[2]), jnp.bfloat16),
        in_specs=[vmem] * 4,
        out_specs=vmem,
        cost_estimate=pl.CostEstimate(flops=1_000, bytes_accessed=600_000, transcendentals=0),
        name="pack",
    )(rk, rv, pk, pv)


def shards_kernel(adapter_ref, parts_ref):
    width = adapter_ref.shape[1]
    parts_ref[0] = jnp.zeros(parts_ref.shape[1:], jnp.bfloat16)
    parts_ref[0, :, :width] = adapter_ref[...].astype(jnp.bfloat16)
    shard = parts_ref[0]
    for i in range(1, parts_ref.shape[0]):
        parts_ref[i] = shard


def shards(adapter, n_fsdp):
    vmem = pl.BlockSpec(memory_space=pltpu.VMEM)
    return pl.pallas_call(
        shards_kernel,
        out_shape=jax.ShapeDtypeStruct((n_fsdp, RANK, LANES), jnp.bfloat16),
        in_specs=[vmem],
        out_specs=vmem,
        cost_estimate=pl.CostEstimate(flops=1_000, bytes_accessed=300_000, transcendentals=0),
        name="shards",
    )(adapter)


def unpack_kernel(kv_ref, rk_ref, rv_ref, pk_ref, pv_ref):
    half = rk_ref.shape[2]
    rk_ref[0] = kv_ref[PRE:, :half]
    rv_ref[0] = kv_ref[PRE:, half:]
    pk_ref[0] = kv_ref[:PRE, :half]
    pv_ref[0] = kv_ref[:PRE, half:]


def unpack(kv_sum):
    vmem = pl.BlockSpec(memory_space=pltpu.VMEM)
    half = kv_sum.shape[1] // 2
    return pl.pallas_call(
        unpack_kernel,
        out_shape=(
            jax.ShapeDtypeStruct((1, TOK, half), jnp.bfloat16),
            jax.ShapeDtypeStruct((1, TOK, half), jnp.bfloat16),
            jax.ShapeDtypeStruct((1, PRE, half), jnp.bfloat16),
            jax.ShapeDtypeStruct((1, PRE, half), jnp.bfloat16),
        ),
        in_specs=[vmem],
        out_specs=[vmem] * 4,
        cost_estimate=pl.CostEstimate(flops=1_000, bytes_accessed=600_000, transcendentals=0),
        name="unpack",
    )(kv_sum)


def norm_kernel(parts_ref, owned_ref, squares_ref):
    owned = jnp.sum(parts_ref[...].astype(jnp.float32), axis=0)
    owned_ref[...] = owned
    squares = jnp.sum(jnp.sum(owned * owned, axis=0, keepdims=True), axis=1, keepdims=True)
    squares_ref[...] = jnp.broadcast_to(squares[None], squares_ref.shape)


def norm(parts, copies):
    vmem = pl.BlockSpec(memory_space=pltpu.VMEM)
    return pl.pallas_call(
        norm_kernel,
        out_shape=(
            jax.ShapeDtypeStruct(parts.shape[1:], jnp.float32),
            jax.ShapeDtypeStruct((copies, 1, LANES), jnp.float32),
        ),
        in_specs=[vmem],
        out_specs=[vmem] * 2,
        cost_estimate=pl.CostEstimate(flops=100_000, bytes_accessed=100_000, transcendentals=0),
        name="norm",
    )(parts)


def adam_update_of(gradient, first_term, second_term, clip_factor):
    scaled = gradient * clip_factor
    moment = first_term + (1.0 - beta_first) * scaled
    second_new = second_term + (1.0 - beta_second) * scaled * scaled
    return moment / first_fix / (jnp.sqrt(second_new / second_fix) + adam_eps)


def swap(x, axis):
    return lax.all_to_all(x, axis, 0, 0, tiled=True)


def on_device(
    queries, resp_keys, response_values, rotated_prompt_keys, prompt_value_rows,
    attention_output_gradient, output_grad, advantages, lengths, tree_mask,
    adapter, first_moment, second_moment,
):
    n_resp = lax.axis_size("resp")
    n_fsdp = lax.axis_size("fsdp")
    place = lax.axis_index("resp").astype(jnp.int32).reshape(1)
    own_kv = pack(resp_keys, response_values, rotated_prompt_keys, prompt_value_rows)
    kv = lax.all_gather(own_kv, "resp", axis=0, tiled=True)
    gathered = swap(shards(adapter, n_fsdp), "fsdp")
    out_cot, low_t, low_in, qs, gs, gt, blocks, bias = prepare(
        place, lengths, tree_mask[0], advantages, gathered, queries[0], output_grad[0],
        attention_output_gradient[0],
    )
    parts, turned, kv_grad = attend(
        blocks, bias, qs, gs, gt, low_t, low_in, out_cot, kv, n_fsdp, n_resp
    )
    kv_sum = lax.psum_scatter(kv_grad, "resp", scatter_dimension=0, tiled=True)
    arrived = swap(hold(parts), "fsdp")
    q_grad = turn(turned)
    arrived, q_grad = lax.optimization_barrier((arrived, q_grad))
    group = jnp.sum(arrived.astype(jnp.float32), axis=0).astype(jnp.bfloat16)
    owned, squares = norm(swap(jnp.broadcast_to(group, (n_resp,) + group.shape), "resp"), n_fsdp)
    owned, first_term, second_term = lax.optimization_barrier(
        (owned, beta_first * first_moment, beta_second * second_moment)
    )
    squares = swap(squares, "fsdp")
    sums = unpack(kv_sum)
    squares, sums = lax.optimization_barrier((squares, sums))
    total = jnp.sum(squares, axis=0)[:, : adapter.shape[1]]
    clip_factor = max_norm / jnp.maximum(jnp.sqrt(total), max_norm)
    update = adam_update_of(owned[:, : adapter.shape[1]], first_term, second_term, clip_factor)
    return (q_grad[None],) + tuple(sums) + (update,)


def solution(mesh):
    tokens = P("fsdp", "resp", None)
    columns = P(None, "fsdp")
    in_specs = (
        (tokens,) * 7
        + (P("fsdp", "resp"), P("fsdp", None), P("fsdp", None, None))
        + (columns,) * 3
    )
    out_specs = (tokens,) * 5 + (columns,)
    return jax.shard_map(
        on_device, mesh=mesh, in_specs=in_specs, out_specs=out_specs, check_vma=False
    )
```
